128 devices in a mesh: pipe: 2 (over y_lo), expert: 8 (over z, core), dp: 8 (over y_hi, x).
Axes of the slice: x: 4, y: 4 (y_hi: 2, y_lo: 2; y = y_hi * 2 + y_lo), z: 4, core: 2. Of those that a mesh axis runs over, the one named last changes fastest.
Arguments:
- activations: bfloat16 [2, 2, 4096, 4096], P('pipe', None, ('expert', 'dp')), may hold values from -6 to 6
- cotangent: bfloat16 [2, 4096, 4096], P(None, ('expert', 'dp')), may hold values from -6 to 6
- routes: int32 [2, 2, 4096, 2], P('pipe', None, ('expert', 'dp')), may hold values from 0 to 7, all different within a row; in each aligned block of 64 rows (0 to 63, 64 to 127, ..., all dimensions but the last counted through in order) at most 24 rows name the same one
- route_weights: float32 [2, 2, 4096, 2], P('pipe', None, ('expert', 'dp')), may hold values from 0.1 to 1
- placement: int32 [2, 8], P('pipe'), may hold values from 0 to 7, each once within a row
- gate_weight: bfloat16 [2, 8, 4096, 768], P('pipe', 'expert'), may hold values from -0.09375 to 0.09375
- up_weight: bfloat16 [2, 8, 4096, 768], P('pipe', 'expert'), may hold values from -0.09375 to 0.09375
- down_weight: bfloat16 [2, 8, 4096, 768], P('pipe', 'expert'), may hold values from -0.21875 to 0.21875
Outputs:
- input_grads: bfloat16 [2, 2, 4096, 4096], P('pipe', None, ('expert', 'dp'))
- gate_grads: bfloat16 [2, 8, 4096, 768], P('pipe', 'expert', 'dp')
- up_grads: bfloat16 [2, 8, 4096, 768], P('pipe', 'expert', 'dp')
- down_grads: bfloat16 [2, 8, 4096, 768], P('pipe', 'expert', 'dp')
The draws below stay inside these ranges and needn't reach their ends.
Inputs may be any that keep to these rules, and one draw needn't show every extreme that they name: `routes`: each token's 2 ids differ; among the 64 tokens of one device, section and micro-batch no expert is named more than 24 times, a bound that some block reaches. `placement`: each row is a permutation.
All inputs are finite; a program needn't handle non-finite values.
Results may differ from the reference program's by a relative error of at most 0.017.
Values may be sent and summed in bfloat16 or wider, within the bound.
A program may use at most 128 MiB of HBM per device.

```python
import math
import jax
import jax.numpy as jnp
import numpy as np
from jax import lax

D = 4096
FF = 768
TOP = 2
MB = 2
TOK_DEV = 64
EXPERTS = 8
CAP = 24
TOKENS = 4096
N_PIPE = 2
N_EXPERT = 8
N_DP = 8


def block_levels(rng, shape, shards, smallest, top_value):
    factor_of, own = 1.0, jax.random.fold_in(rng, 6)
    for dim, blocks in shards:
        steps = jnp.exp(jax.random.uniform(jax.random.fold_in(own, dim), (blocks,), jnp.float32, smallest / len(shards), top_value / len(shards)))
        factor_of = factor_of * jnp.repeat(steps, shape[dim] // blocks).reshape([-1 if axis == dim else 1 for axis in range(len(shape))])
    return factor_of


def assign_block(own_key, own, number, rows, number_of, top, limit, slope):
    ranking = jax.random.permutation(own_key, number_of)
    crowded, ordinary = shares(number_of, rows * top, limit, slope, True), shares(number_of, rows * top, limit, slope, False)
    places = jnp.arange(number_of)

    def named(tallies, turn):
        used = int((tallies > 0).sum())
        fixed = max(1, used // 4)
        moved = fixed + (places - fixed + turn * (used - fixed)) % max(1, number_of - fixed)
        return jnp.zeros((number_of,), jnp.int32).at[ranking[jnp.where(places < fixed, places, moved)]].set(jnp.asarray(tallies, jnp.int32))

    tallies = jnp.where(number % 4 == 0, named(crowded, number // 4), named(ordinary, number - number // 4 - 1))
    mixed = jax.random.permutation(jax.random.fold_in(own, 3), number_of)
    source_of, receiver = mixed[0:number_of // 2 * 2:2], mixed[1:number_of // 2 * 2:2]
    margin = jnp.minimum(tallies[source_of] - 1, limit - tallies[receiver]) // 2
    margin = jnp.where((source_of == ranking[0]) | (receiver == ranking[0]) | (tallies[receiver] == 0), 0, jnp.maximum(margin, 0))
    moved = jax.random.randint(jax.random.fold_in(own, 4), (number_of // 2,), 0, 1 << 20) % (margin + 1)
    tallies = tallies.at[source_of].add(-moved).at[receiver].add(moved)
    items = jnp.searchsorted(jnp.cumsum(tallies), jnp.arange(rows * top), side="right").astype(jnp.int32)
    grid = items.reshape(top, rows).T
    grid = grid[jax.random.permutation(jax.random.fold_in(own, 1), rows)]
    turn = jax.random.randint(jax.random.fold_in(own, 2), (rows, 1), 0, top)
    return jnp.take_along_axis(grid, (jnp.arange(top)[None, :] + turn) % top, axis=1)


def shares(number_of, total, bound, slope, full):
    weights = [(1 << 20) // math.isqrt(rank ** slope) + 1 for rank in range(1, number_of + 1)]
    largest = bound if full else min(bound, max(-(-total // number_of), total * weights[0] // sum(weights)))
    least = 1 if total - largest >= number_of - 1 else 0
    given, rest = [largest] + [least] * (number_of - 1), total - largest - least * (number_of - 1)
    while rest > 0:
        free = [i for i in range(1, number_of) if given[i] < largest] or [i for i in range(1, number_of) if given[i] < bound]
        whole, budget = sum([weights[i] for i in free]), rest
        for i in free:
            more = min(bound - given[i], max(1, budget * weights[i] // whole), rest)
            given[i] = given[i] + more
            rest = rest - more
    return np.array(given)


def gaussian(stream_key, shape, width, most, shards=(), kind=jnp.bfloat16):
    drawn = width * jax.random.normal(stream_key, shape, jnp.float32)
    if shards:
        drawn = drawn * block_levels(stream_key, shape, shards, -0.22, 0.18)
    return jnp.clip(drawn, -most, most).astype(kind)


def setup_inputs(seed: int = 0) -> dict:
    key_list = jax.random.split(jax.random.key(seed), 9)
    activations = gaussian(key_list[0], (N_PIPE, MB, TOKENS, D), 1.0, 6.0, ((0, 2), (2, 64)))
    cotangent = gaussian(key_list[1], (MB, TOKENS, D), 1.0, 6.0, ((1, 64),))
    routes_keys = jax.random.split(jax.random.fold_in(key_list[2], 1), N_PIPE * MB * TOKENS // TOK_DEV)
    routes_turns = jax.random.permutation(jax.random.fold_in(key_list[2], 3), N_PIPE * MB * TOKENS // TOK_DEV)
    routes = jax.vmap(lambda own, number: assign_block(jax.random.fold_in(key_list[2], 2), own, number, TOK_DEV, EXPERTS, TOP, CAP, 2))(routes_keys, routes_turns).reshape((N_PIPE, MB, TOKENS, TOP))
    route_weights = jnp.clip(jnp.exp(math.log(1.0) - 2.3025851 * jax.random.uniform(key_list[3], (N_PIPE, MB, TOKENS, TOP), jnp.float32) ** block_levels(key_list[3], (N_PIPE, MB, TOKENS, TOP), ((0, 2), (2, 64)), -0.2, 0.2)), 0.1, 1.0)
    placement = jax.vmap(lambda own: jax.random.permutation(own, EXPERTS))(jax.random.split(key_list[4], N_PIPE)).reshape((N_PIPE, EXPERTS)).astype(jnp.int32)
    gate_weight = gaussian(key_list[5], (N_PIPE, EXPERTS, D, FF), D ** -0.5, 0.09375, ((0, 2), (1, 8)))
    up_weight = gaussian(key_list[6], (N_PIPE, EXPERTS, D, FF), D ** -0.5, 0.09375, ((0, 2), (1, 8)))
    down_weight = gaussian(key_list[7], (N_PIPE, EXPERTS, D, FF), FF ** -0.5, 0.21875, ((0, 2), (1, 8)))
    return {"activations": activations, "cotangent": cotangent, "routes": routes, "route_weights": route_weights, "placement": placement, "gate_weight": gate_weight, "up_weight": up_weight, "down_weight": down_weight}


def expert_backward(rows_in, rows_cot, w_gate, w_up, w_down):
    pre_gate = jnp.dot(rows_in, w_gate, preferred_element_type=jnp.float32)
    pre_up = jnp.dot(rows_in, w_up, preferred_element_type=jnp.float32)
    sigmoid_gate = jax.nn.sigmoid(pre_gate)
    active = pre_gate * sigmoid_gate
    hidden = (active * pre_up).astype(jnp.bfloat16)
    grad_hidden = jnp.dot(rows_cot, w_down, preferred_element_type=jnp.float32)
    grad_gate = (grad_hidden * pre_up * sigmoid_gate * (1.0 + pre_gate * (1.0 - sigmoid_gate))).astype(jnp.bfloat16)
    grad_up = (grad_hidden * active).astype(jnp.bfloat16)
    grad_rows = (jnp.dot(grad_gate, w_gate.T, preferred_element_type=jnp.float32)
                 + jnp.dot(grad_up, w_up.T, preferred_element_type=jnp.float32)).astype(jnp.bfloat16)
    return grad_rows, hidden, grad_gate, grad_up


def replica_sum(left_rows, right_rows):
    block_shape = (MB, N_EXPERT, N_DP, CAP)
    left_five = left_rows.reshape(block_shape + (left_rows.shape[-1],)).astype(jnp.float32)
    right_five = right_rows.reshape(block_shape + (right_rows.shape[-1],)).astype(jnp.float32)
    per_replica = jnp.einsum("mijcd,mijcf->jdf", left_five, right_five)
    rounded = lax.optimization_barrier(per_replica.astype(jnp.bfloat16))
    return jnp.sum(rounded.astype(jnp.float32), axis=0).astype(jnp.bfloat16)


def reference(activations, cotangent, routes, route_weights, placement, gate_weight, up_weight, down_weight):
    blocks = N_EXPERT * N_DP
    assign_count = TOK_DEV * TOP
    row_count = blocks * CAP
    expert_ids = jnp.arange(EXPERTS, dtype=jnp.int32)
    owners = jnp.repeat(jnp.arange(TOKENS, dtype=jnp.int32).reshape(blocks, TOK_DEV), TOP, axis=1)
    block_ids = jnp.arange(blocks, dtype=jnp.int32)[:, None]
    upstream = cotangent
    input_list = [None] * N_PIPE
    gate_list = [None] * N_PIPE
    up_list = [None] * N_PIPE
    down_list = [None] * N_PIPE
    for section_index in range(N_PIPE - 1, -1, -1):
        inverse = jnp.zeros((EXPERTS,), jnp.int32).at[placement[section_index]].set(expert_ids)
        tables = []
        scales = []
        for micro_index in range(MB):
            slot_ids = inverse[routes[section_index, micro_index]].reshape(blocks, assign_count)
            onehot = (slot_ids[:, :, None] == expert_ids).astype(jnp.int32)
            slot_rank = jnp.sum((jnp.cumsum(onehot, axis=1) - 1) * onehot, axis=2)
            flat_index = ((slot_ids * blocks + block_ids) * CAP + slot_rank).reshape(-1)
            token_table = jnp.full((EXPERTS * row_count,), TOKENS, jnp.int32).at[flat_index].set(owners.reshape(-1))
            slot_scale = jnp.zeros((EXPERTS * row_count,), jnp.float32).at[flat_index].set(route_weights[section_index, micro_index].reshape(-1))
            tables.append(token_table.reshape(EXPERTS, row_count))
            scales.append(slot_scale.reshape(EXPERTS, row_count))
        token_table = jnp.stack(tables, axis=1)
        slot_scale = jnp.stack(scales, axis=1)
        padding = jnp.zeros((MB, 1, D), jnp.bfloat16)
        inputs_pad = jnp.concatenate([activations[section_index], padding], axis=1)
        cot_pad = jnp.concatenate([upstream, padding], axis=1)

        def per_expert(packed):
            table_one, scale_one, w_gate, w_up, w_down = packed
            rows_in = jnp.stack([jnp.take(inputs_pad[micro_index], table_one[micro_index], axis=0) for micro_index in range(MB)])
            rows_cot = jnp.stack([jnp.take(cot_pad[micro_index], table_one[micro_index], axis=0) for micro_index in range(MB)])
            rows_cot = (scale_one[:, :, None] * rows_cot.astype(jnp.float32)).astype(jnp.bfloat16)
            rows_in = rows_in.reshape(MB * row_count, D)
            rows_cot = rows_cot.reshape(MB * row_count, D)
            grad_rows, hidden, grad_gate, grad_up = expert_backward(rows_in, rows_cot, w_gate, w_up, w_down)
            return (grad_rows.reshape(MB, row_count, D), replica_sum(rows_in, grad_gate),
                    replica_sum(rows_in, grad_up), replica_sum(rows_cot, hidden))

        grad_rows, gate_part, up_part, down_part = lax.map(
            per_expert, (token_table, slot_scale, gate_weight[section_index], up_weight[section_index], down_weight[section_index]))
        results = []
        for micro_index in range(MB):
            summed = jnp.zeros((TOKENS + 1, D), jnp.float32).at[token_table[:, micro_index].reshape(-1)].add(
                grad_rows[:, micro_index].reshape(-1, D).astype(jnp.float32))
            results.append((upstream[micro_index].astype(jnp.float32) + summed[:TOKENS]).astype(jnp.bfloat16))
        upstream = jnp.stack(results)
        input_list[section_index] = upstream
        gate_list[section_index] = gate_part
        up_list[section_index] = up_part
        down_list[section_index] = down_part
    return jnp.stack(input_list), jnp.stack(gate_list), jnp.stack(up_list), jnp.stack(down_list)
```

```python
import functools

import jax
import jax.numpy as jnp
from jax import lax
from jax.experimental import pallas as pl
from jax.experimental.pallas import tpu as pltpu
from jax.sharding import PartitionSpec as P

CAP = 24
NX = 4
F32 = jnp.float32
BF16 = jnp.bfloat16


def nt(left, right):
    return lax.dot_general(left, right, (((1,), (1,)), ((), ())), preferred_element_type=F32)


def nn(left, right):
    return jnp.dot(left, right, preferred_element_type=F32)


def mega(
    x_ref, cot_ref, posr_ref, posc_ref, rw_ref, wg_hbm, wu_hbm, wd_hbm,
    ig_ref, og_ref, ou_ref, od_ref,
    wg, wu, wd, xs, gs, xr, dr, ret, up, xsl, dsl, hh, aa, uu, yrecv,
    sel, selt, scale, a_acc, u_acc, q_acc,
    wsem, xss, xrs, gss, grs, dss, drs, lsem, pss, prs,
    xa_s, xa_r, da_s, da_r, h_s, h_r, ag_s, ag_r, au_s, au_r, ys, yr,
):
    p = lax.axis_index("pipe")
    me = lax.axis_index("expert")
    j = lax.axis_index("dp")
    ne = lax.axis_size("expert")
    ndp = lax.axis_size("dp")
    ny = ndp // NX
    x = lax.rem(j, NX)
    yh = j // NX
    last = lax.axis_size("pipe") - 1
    tokens, d = x_ref.shape
    rows = sel.shape[0]
    blk = rows // ne
    ff = wg.shape[2]
    cw = d // NX
    cp = cw // ny
    is_last = p == last

    def at_z(e):
        return (p, e, j)

    def at_x(k):
        return (p, me, yh * NX + k)

    def mesh_copy(src, dst, s, r, dev):
        return pltpu.make_async_remote_copy(
            src_ref=src, dst_ref=dst, send_sem=s, recv_sem=r,
            device_id=dev, device_id_type=pl.DeviceIdType.MESH,
        )

    y_peer = (p, me, lax.rem(yh + 1, ny) * NX + x)
    p_peer = (last - p, me, j)

    def w_copies(t, k):
        src, dst = ((wg_hbm, wg), (wu_hbm, wu), (wd_hbm, wd))[t]
        return [
            pltpu.make_async_copy(
                src.at[pl.ds(h * (d // ny) + k * cp, cp)],
                dst.at[k, pl.ds(h * cp, cp)],
                wsem.at[t, k, h],
            )
            for h in range(ny)
        ]

    for t in range(3):
        for k in range(NX):
            for c in w_copies(t, k):
                c.start()

    barrier = pltpu.get_barrier_semaphore()
    peers = [at_z(lax.rem(me + o, ne)) for o in range(1, ne)]
    peers += [at_x(lax.rem(x + o, NX)) for o in range(1, NX)]
    peers += [y_peer, p_peer]
    for dev in peers:
        pl.semaphore_signal(barrier, inc=1, device_id=dev, device_id_type=pl.DeviceIdType.MESH)

    r_iota = lax.broadcasted_iota(jnp.int32, (rows, tokens), 0)
    hit0 = r_iota == posr_ref[0:1, :]
    hit1 = r_iota == posr_ref[1:2, :]
    sel[...] = jnp.where(hit0 | hit1, 1.0, 0.0).astype(BF16)
    weight = jnp.where(hit0, rw_ref[0:1, :], 0.0) + jnp.where(hit1, rw_ref[1:2, :], 0.0)
    scale[...] = jnp.broadcast_to(jnp.sum(weight, axis=1, keepdims=True), scale.shape)
    c_iota = lax.broadcasted_iota(jnp.int32, (tokens, rows), 1)
    selt[...] = jnp.where(
        (c_iota == posc_ref[:, 0:1]) | (c_iota == posc_ref[:, 1:2]), 1.0, 0.0
    ).astype(BF16)

    pl.semaphore_wait(barrier, len(peers))

    def my_rows(e):
        return pl.ds(pl.multiple_of(e * blk, 16), blk)

    def z_sends(stage, land, ss, rs, k):
        out = []
        for o in range(1, ne):
            e = lax.rem(me + o, ne)
            out.append(
                mesh_copy(
                    stage.at[k, my_rows(e)], land.at[k, my_rows(me)],
                    ss.at[k, o], rs.at[k, o], at_z(e),
                )
            )
        return out

    def z_own(stage, land, ss, k):
        return pltpu.make_async_copy(
            stage.at[k, my_rows(me)], land.at[k, my_rows(me)], ss.at[k, 0]
        )

    def z_start(stage, land, ss, rs, k):
        for c in z_sends(stage, land, ss, rs, k):
            c.start()
        z_own(stage, land, ss, k).start()

    def z_recv(stage, land, ss, rs, k):
        for o in range(1, ne):
            e = lax.rem(me + ne - o, ne)
            mesh_copy(
                stage.at[k, my_rows(e)], land.at[k, my_rows(e)],
                ss.at[k, o], rs.at[k, o], at_z(e),
            ).wait_recv()
        z_own(stage, land, ss, k).wait()

    def z_done(stage, land, ss, rs, k):
        for c in z_sends(stage, land, ss, rs, k):
            c.wait_send()

    def piece(k, h):
        return pl.ds(pl.multiple_of(h * (d // ny) + k * cp, cp), cp)

    def chunk_of(ref, k):
        return jnp.concatenate([ref[:, piece(k, h)] for h in range(ny)], axis=1)

    def send_scaled(k):
        picked = nn(sel[...], up[k])
        gs[k] = (scale[:, 0:1] * picked).astype(BF16)
        z_start(gs, dr, gss, grs, k)

    @pl.loop(0, NX)
    def _(k):
        xs[k] = nn(sel[...], chunk_of(x_ref, k)).astype(BF16)
        z_start(xs, xr, xss, xrs, k)

        @pl.when(is_last)
        def _():
            up[k] = chunk_of(cot_ref, k)
            send_scaled(k)

    def share_copy(src, dst, ss, rs, k):
        return mesh_copy(src.at[k], dst.at[x], ss.at[k], rs.at[x], at_x(k))

    def share_local(src, dst, k, n):
        return pltpu.make_async_copy(src.at[k], dst.at[k], lsem.at[n])

    def share_start(src, dst, ss, rs, k, n):
        @pl.when(k != x)
        def _():
            share_copy(src, dst, ss, rs, k).start()

        @pl.when(k == x)
        def _():
            share_local(src, dst, k, n).start()

    def share_wait(src, dst, ss, rs, n):
        for o in range(1, NX):
            k = lax.rem(x + o, NX)
            share_copy(src, dst, ss, rs, k).wait_send()
            mesh_copy(src.at[k], dst.at[k], ss.at[k], rs.at[k], at_x(k)).wait_recv()
        share_local(src, dst, x, n).wait()

    def rows_of(s):
        return pl.ds(pl.multiple_of(s * rows, 16), rows)

    def gather(buf, ss, rs):
        return [
            mesh_copy(
                buf.at[rows_of(x)], buf.at[rows_of(x)], ss.at[o], rs.at[o],
                at_x(lax.rem(x + o, NX)),
            )
            for o in range(1, NX)
        ]

    def gather_start(buf, ss, rs):
        for c in gather(buf, ss, rs):
            c.start()

    def gather_wait(buf, ss, rs):
        for o, c in zip(range(1, NX), gather(buf, ss, rs)):
            c.wait_send()
            s = lax.rem(x + NX - o, NX)
            mesh_copy(
                buf.at[rows_of(s)], buf.at[rows_of(s)], ss.at[o], rs.at[o], at_x(s)
            ).wait_recv()

    tile = 256 if ff % 256 == 0 else ff

    a_acc[...] = jnp.zeros_like(a_acc)
    u_acc[...] = jnp.zeros_like(u_acc)
    q_acc[...] = jnp.zeros_like(q_acc)

    def wait_w(t, k):
        for c in w_copies(t, k):
            c.wait()

    @pl.loop(0, NX)
    def _(k):
        z_recv(xs, xr, xss, xrs, k)
        share_start(xr, xsl, xa_s, xa_r, k, 0)
        wait_w(0, k)
        wait_w(1, k)

        @pl.loop(0, ff // tile)
        def _(n):
            c = pl.ds(pl.multiple_of(n * tile, tile), tile)
            a_acc[:, c] += nn(xr[k], wg[k, :, c])
            u_acc[:, c] += nn(xr[k], wu[k, :, c])

    a = a_acc[...]
    hh[rows_of(x), :] = (a * jax.nn.sigmoid(a) * u_acc[...]).astype(BF16)
    gather_start(hh, h_s, h_r)

    def pipe_copy(k):
        return mesh_copy(up.at[k], up.at[k], pss.at[k], prs.at[k], p_peer)

    def take_dr(k):
        z_recv(gs, dr, gss, grs, k)
        share_start(dr, dsl, da_s, da_r, k, 1)
        wait_w(2, k)

        @pl.loop(0, ff // tile)
        def _(n):
            c = pl.ds(pl.multiple_of(n * tile, tile), tile)
            q_acc[:, c] += nn(dr[k], wd[k, :, c])

    @pl.loop(0, NX + 1)
    def _(k):
        @pl.when(jnp.logical_not(is_last) & (k < NX))
        def _():
            pipe_copy(k).wait_recv()
            send_scaled(k)

        @pl.when(k > 0)
        def _():
            take_dr(k - 1)

    a = a_acc[...]
    sg = jax.nn.sigmoid(a)
    q = q_acc[...]
    aa[rows_of(x), :] = (q * u_acc[...] * sg * (1.0 + a * (1.0 - sg))).astype(BF16)
    uu[rows_of(x), :] = (q * (a * sg)).astype(BF16)
    gather_start(aa, ag_s, ag_r)
    gather_start(uu, au_s, au_r)

    ct = 256 if cw % 256 == 0 else cw

    @pl.loop(0, NX)
    def _(k):
        z_done(xs, xr, xss, xrs, k)
        ga = aa[rows_of(x), :]
        gu = uu[rows_of(x), :]

        @pl.loop(0, cw // ct)
        def _(n):
            c = pl.ds(pl.multiple_of(n * ct, ct), ct)
            xs[k, :, c] = (nt(ga, wg[k, c, :]) + nt(gu, wu[k, c, :])).astype(BF16)

        z_start(xs, ret, dss, drs, k)

    @pl.loop(0, NX)
    def _(k):
        z_recv(xs, ret, dss, drs, k)
        total = (up[k].astype(F32) + nn(selt[...], ret[k])).astype(BF16)
        for h in range(ny):
            ig_ref[:, piece(k, h)] = total[:, h * cp : (h + 1) * cp]

        @pl.when(is_last)
        def _():
            up[k] = total
            pipe_copy(k).start()

    kh = wg.shape[2] // rows if wg.shape[2] % rows == 0 else 1

    def transposed(src, dst):
        for s in range(NX):
            for h in range(ny):
                dst[s // kh, h * cp : (h + 1) * cp, (s % kh) * rows : (s % kh + 1) * rows] = (
                    jnp.transpose(src[s, :, h * cp : (h + 1) * cp])
                )

    def product(lhs, rhs, h, n):
        c = pl.ds(pl.multiple_of(n * tile, tile), tile)
        r = pl.ds(pl.multiple_of(h * cp, cp), cp)
        acc = nn(lhs[0, r, :], rhs[0 : kh * rows, c])
        for m in range(1, NX // kh):
            acc += nn(lhs[m, r, :], rhs[m * kh * rows : (m + 1) * kh * rows, c])
        return acc

    def y_copy(t):
        return mesh_copy(wd.at[t, pl.ds(0, cp)], yrecv.at[t], ys.at[t], yr.at[t], y_peer)

    def for_peer(t, lhs, rhs):
        @pl.loop(0, ff // tile)
        def _(n):
            c = pl.ds(pl.multiple_of(n * tile, tile), tile)
            wd[t, 0:cp, c] = product(lhs, rhs, lax.rem(yh + 1, ny), n).astype(BF16)

        y_copy(t).start()

    def for_me(t, lhs, rhs, out):
        y_copy(t).wait()

        @pl.loop(0, ff // tile)
        def _(n):
            c = pl.ds(pl.multiple_of(n * tile, tile), tile)
            out[:, c] = (product(lhs, rhs, yh, n) + yrecv[t, :, c].astype(F32)).astype(BF16)

    share_wait(dr, dsl, da_s, da_r, 1)
    transposed(dsl, wu)
    gather_wait(hh, h_s, h_r)
    for_peer(0, wu, hh)
    share_wait(xr, xsl, xa_s, xa_r, 0)
    transposed(xsl, wg)
    gather_wait(aa, ag_s, ag_r)
    for_peer(1, wg, aa)
    gather_wait(uu, au_s, au_r)
    for_peer(2, wg, uu)
    for_me(0, wu, hh, od_ref)
    for_me(1, wg, aa, og_ref)
    for_me(2, wg, uu, ou_ref)

    @pl.loop(0, NX)
    def _(k):
        z_done(gs, dr, gss, grs, k)
        z_done(xs, ret, dss, drs, k)

        @pl.when(is_last)
        def _():
            pipe_copy(k).wait_send()


def slots_of(routes, placement):
    micro, count, top = routes.shape
    experts = placement.shape[0]
    match = routes.reshape(micro, count * top)[:, :, None] == placement
    slot = jnp.sum(jnp.where(match, jnp.arange(experts, dtype=jnp.int32), 0), axis=2)
    order = jnp.arange(count * top)
    before = order[None, :] < order[:, None]
    same = slot[:, :, None] == slot[:, None, :]
    rank = jnp.sum((same & before).astype(jnp.int32), axis=2)
    place = (slot * micro + jnp.arange(micro, dtype=jnp.int32)[:, None]) * CAP + rank
    return place.reshape(micro * count, top)


def local(
    activations, cotangent, routes, route_weights, placement, gate_weight, up_weight, down_weight
):
    ne = lax.axis_size("expert")
    ny = lax.axis_size("dp") // NX
    _, micro, count, d = activations.shape
    tokens = micro * count
    ff = gate_weight.shape[3]
    rows = ne * micro * CAP
    cw = d // NX
    cp = cw // ny
    place = slots_of(routes[0], placement[0])
    vm = functools.partial(pl.BlockSpec, memory_space=pltpu.VMEM)
    hbm = functools.partial(pl.BlockSpec, memory_space=pl.ANY)
    dma = pltpu.SemaphoreType.DMA
    wide = pltpu.VMEM((NX, rows, cw), BF16)
    tall = pltpu.VMEM((NX * rows, ff), BF16)
    weight = pltpu.VMEM((NX, cw, ff), BF16)
    acc = pltpu.VMEM((rows, ff), F32)
    outs = pl.pallas_call(
        mega,
        out_shape=(
            jax.ShapeDtypeStruct((tokens, d), BF16),
            jax.ShapeDtypeStruct((cp, ff), BF16),
            jax.ShapeDtypeStruct((cp, ff), BF16),
            jax.ShapeDtypeStruct((cp, ff), BF16),
        ),
        in_specs=[vm()] * 5 + [hbm()] * 3,
        out_specs=(vm(),) * 4,
        scratch_shapes=[
            weight, weight, weight,
            wide, wide, wide, wide, wide,
            pltpu.VMEM((NX, tokens, cw), BF16),
            wide, wide,
            tall, tall, tall,
            pltpu.VMEM((3, cp, ff), BF16),
            pltpu.VMEM((rows, tokens), BF16),
            pltpu.VMEM((tokens, rows), BF16),
            pltpu.VMEM((rows, 128), F32),
            acc, acc, acc,
            dma((3, NX, ny)),
            dma((NX, ne)), dma((NX, ne)), dma((NX, ne)), dma((NX, ne)),
            dma((NX, ne)), dma((NX, ne)),
            dma((2,)),
            dma((NX,)), dma((NX,)),
            dma((NX,)), dma((NX,)), dma((NX,)), dma((NX,)),
            dma((NX,)), dma((NX,)), dma((NX,)), dma((NX,)), dma((NX,)), dma((NX,)),
            dma((3,)), dma((3,)),
        ],
        compiler_params=pltpu.CompilerParams(
            collective_id=0, has_side_effects=True, vmem_limit_bytes=63 * 2**20
        ),
        cost_estimate=pl.CostEstimate(
            flops=20 * 10**9, bytes_accessed=24 * 10**6, transcendentals=10**6
        ),
    )(
        activations.reshape(tokens, d),
        cotangent.reshape(tokens, d),
        place.T,
        place,
        route_weights.reshape(tokens, -1).T,
        gate_weight[0, 0],
        up_weight[0, 0],
        down_weight[0, 0],
    )
    return (
        outs[0].reshape(1, micro, count, d),
        outs[1][None, None],
        outs[2][None, None],
        outs[3][None, None],
    )


def solution(mesh):
    blocks = ("expert", "dp")
    placed = (
        P("pipe", None, blocks, None),
        P(None, blocks, None),
        P("pipe", None, blocks, None),
        P("pipe", None, blocks, None),
        P("pipe", None),
        P("pipe", "expert", None, None),
        P("pipe", "expert", None, None),
        P("pipe", "expert", None, None),
    )
    return jax.shard_map(
        local,
        mesh=mesh,
        in_specs=placed,
        out_specs=(
            P("pipe", None, blocks, None),
            P("pipe", "expert", "dp", None),
            P("pipe", "expert", "dp", None),
            P("pipe", "expert", "dp", None),
        ),
        check_vma=False,
    )
```

```python
import functools

import jax
import jax.numpy as jnp
from jax import lax
from jax.experimental import pallas as pl
from jax.experimental.pallas import tpu as pltpu
from jax.sharding import PartitionSpec as P

CAP = 24
NX = 4
F32 = jnp.float32
BF16 = jnp.bfloat16


def nt(left, right):
    return lax.dot_general(left, right, (((1,), (1,)), ((), ())), preferred_element_type=F32)


def nn(left, right):
    return jnp.dot(left, right, preferred_element_type=F32)


def mega(
    x_ref, cot_ref, posr_ref, posc_ref, rw_ref, wg_hbm, wu_hbm, wd_hbm,
    ig_ref, og_ref, ou_ref, od_ref,
    wg, wu, wd, xs, gs, xr, dr, ret, up, xsl, dsl, hh, aa, uu, yrecv,
    sel, selt, scale, a_acc, u_acc, q_acc,
    wsem, xss, xrs, gss, grs, dss, drs, lsem, pss, prs,
    xa_s, xa_r, da_s, da_r, h_s, h_r, ag_s, ag_r, au_s, au_r, ys, yr, igs, gos,
):
    p = lax.axis_index("pipe")
    me = lax.axis_index("expert")
    j = lax.axis_index("dp")
    ne = lax.axis_size("expert")
    ndp = lax.axis_size("dp")
    ny = ndp // NX
    x = lax.rem(j, NX)
    yh = j // NX
    last = lax.axis_size("pipe") - 1
    tokens, d = x_ref.shape
    rows = sel.shape[0]
    blk = rows // ne
    ff = wg.shape[2]
    cw = d // NX
    cp = cw // ny
    is_last = p == last

    def at_z(e):
        return (p, e, j)

    def at_x(k):
        return (p, me, yh * NX + k)

    def mesh_copy(src, dst, s, r, dev):
        return pltpu.make_async_remote_copy(
            src_ref=src, dst_ref=dst, send_sem=s, recv_sem=r,
            device_id=dev, device_id_type=pl.DeviceIdType.MESH,
        )

    y_peer = (p, me, lax.rem(yh + 1, ny) * NX + x)
    p_peer = (last - p, me, j)

    def w_copies(t, k):
        src, dst = ((wg_hbm, wg), (wu_hbm, wu), (wd_hbm, wd))[t]
        return [
            pltpu.make_async_copy(
                src.at[pl.ds(h * (d // ny) + k * cp, cp)],
                dst.at[k, pl.ds(h * cp, cp)],
                wsem.at[t, k, h],
            )
            for h in range(ny)
        ]

    for t in range(3):
        for k in range(NX):
            for c in w_copies(t, k):
                c.start()

    barrier = pltpu.get_barrier_semaphore()
    peers = [at_z(lax.rem(me + o, ne)) for o in range(1, ne)]
    peers += [at_x(lax.rem(x + o, NX)) for o in range(1, NX)]
    peers += [y_peer, p_peer]
    for dev in peers:
        pl.semaphore_signal(barrier, inc=1, device_id=dev, device_id_type=pl.DeviceIdType.MESH)

    r_iota = lax.broadcasted_iota(jnp.int32, (rows, tokens), 0)
    hit0 = r_iota == posr_ref[0:1, :]
    hit1 = r_iota == posr_ref[1:2, :]
    sel[...] = jnp.where(hit0 | hit1, 1.0, 0.0).astype(BF16)
    weight = jnp.where(hit0, rw_ref[0:1, :], 0.0) + jnp.where(hit1, rw_ref[1:2, :], 0.0)
    scale[...] = jnp.broadcast_to(jnp.sum(weight, axis=1, keepdims=True), scale.shape)
    c_iota = lax.broadcasted_iota(jnp.int32, (tokens, rows), 1)
    selt[...] = jnp.where(
        (c_iota == posc_ref[:, 0:1]) | (c_iota == posc_ref[:, 1:2]), 1.0, 0.0
    ).astype(BF16)

    pl.semaphore_wait(barrier, len(peers))

    def my_rows(e):
        return pl.ds(pl.multiple_of(e * blk, 16), blk)

    def z_sends(stage, land, ss, rs, k):
        out = []
        for o in range(1, ne):
            e = lax.rem(me + o, ne)
            out.append(
                mesh_copy(
                    stage.at[k, my_rows(e)], land.at[k, my_rows(me)],
                    ss.at[k, o], rs.at[k, o], at_z(e),
                )
            )
        return out

    def z_own(stage, land, ss, k):
        return pltpu.make_async_copy(
            stage.at[k, my_rows(me)], land.at[k, my_rows(me)], ss.at[k, 0]
        )

    def z_start(stage, land, ss, rs, k):
        for c in z_sends(stage, land, ss, rs, k):
            c.start()
        z_own(stage, land, ss, k).start()

    def z_recv(stage, land, ss, rs, k):
        for o in range(1, ne):
            e = lax.rem(me + ne - o, ne)
            mesh_copy(
                stage.at[k, my_rows(e)], land.at[k, my_rows(e)],
                ss.at[k, o], rs.at[k, o], at_z(e),
            ).wait_recv()
        z_own(stage, land, ss, k).wait()

    def z_done(stage, land, ss, rs, k):
        for c in z_sends(stage, land, ss, rs, k):
            c.wait_send()

    def piece(k, h):
        return pl.ds(pl.multiple_of(h * (d // ny) + k * cp, cp), cp)

    def chunk_of(ref, k):
        return jnp.concatenate([ref[:, piece(k, h)] for h in range(ny)], axis=1)

    def send_scaled(k):
        picked = nn(sel[...], up[k])
        gs[k] = (scale[:, 0:1] * picked).astype(BF16)
        z_start(gs, dr, gss, grs, k)

    def turn(step):
        return lax.rem(x + step, NX)

    @pl.loop(0, NX)
    def _(step):
        k = turn(step)
        xs[k] = nn(sel[...], chunk_of(x_ref, k)).astype(BF16)
        z_start(xs, xr, xss, xrs, k)

        @pl.when(is_last)
        def _():
            up[k] = chunk_of(cot_ref, k)
            send_scaled(k)

    def share_copy(src, dst, ss, rs, k):
        return mesh_copy(src.at[k], dst.at[x], ss.at[k], rs.at[x], at_x(k))

    def share_local(src, dst, k, n):
        return pltpu.make_async_copy(src.at[k], dst.at[k], lsem.at[n])

    def share_start(src, dst, ss, rs, k, n):
        @pl.when(k != x)
        def _():
            share_copy(src, dst, ss, rs, k).start()

        @pl.when(k == x)
        def _():
            share_local(src, dst, k, n).start()

    def share_wait(src, dst, ss, rs, n):
        for o in range(1, NX):
            k = lax.rem(x + o, NX)
            share_copy(src, dst, ss, rs, k).wait_send()
            mesh_copy(src.at[k], dst.at[k], ss.at[k], rs.at[k], at_x(k)).wait_recv()
        share_local(src, dst, x, n).wait()

    def rows_of(s):
        return pl.ds(pl.multiple_of(s * rows, 16), rows)

    def gather(buf, ss, rs):
        return [
            mesh_copy(
                buf.at[rows_of(x)], buf.at[rows_of(x)], ss.at[o], rs.at[o],
                at_x(lax.rem(x + o, NX)),
            )
            for o in range(1, NX)
        ]

    def gather_start(buf, ss, rs):
        for c in gather(buf, ss, rs):
            c.start()

    def gather_wait(buf, ss, rs):
        for o, c in zip(range(1, NX), gather(buf, ss, rs)):
            c.wait_send()
            s = lax.rem(x + NX - o, NX)
            mesh_copy(
                buf.at[rows_of(s)], buf.at[rows_of(s)], ss.at[o], rs.at[o], at_x(s)
            ).wait_recv()

    tile = 256 if ff % 256 == 0 else ff

    a_acc[...] = jnp.zeros_like(a_acc)
    u_acc[...] = jnp.zeros_like(u_acc)
    q_acc[...] = jnp.zeros_like(q_acc)

    def wait_w(t, k):
        for c in w_copies(t, k):
            c.wait()

    @pl.loop(0, NX)
    def _(step):
        k = turn(step)
        z_recv(xs, xr, xss, xrs, k)
        share_start(xr, xsl, xa_s, xa_r, k, 0)
        wait_w(0, k)
        wait_w(1, k)

        @pl.loop(0, ff // tile)
        def _(n):
            c = pl.ds(pl.multiple_of(n * tile, tile), tile)
            a_acc[:, c] += nn(xr[k], wg[k, :, c])
            u_acc[:, c] += nn(xr[k], wu[k, :, c])

    a = a_acc[...]
    hh[rows_of(x), :] = (a * jax.nn.sigmoid(a) * u_acc[...]).astype(BF16)
    gather_start(hh, h_s, h_r)

    def pipe_copy(k):
        return mesh_copy(up.at[k], up.at[k], pss.at[k], prs.at[k], p_peer)

    def take_dr(k):
        z_recv(gs, dr, gss, grs, k)
        share_start(dr, dsl, da_s, da_r, k, 1)
        wait_w(2, k)

        @pl.loop(0, ff // tile)
        def _(n):
            c = pl.ds(pl.multiple_of(n * tile, tile), tile)
            q_acc[:, c] += nn(dr[k], wd[k, :, c])

    @pl.loop(0, NX + 1)
    def _(step):
        @pl.when(jnp.logical_not(is_last) & (step < NX))
        def _():
            pipe_copy(turn(step)).wait_recv()
            send_scaled(turn(step))

        @pl.when(step > 0)
        def _():
            take_dr(turn(step + NX - 1))

    a = a_acc[...]
    sg = jax.nn.sigmoid(a)
    q = q_acc[...]
    aa[rows_of(x), :] = (q * u_acc[...] * sg * (1.0 + a * (1.0 - sg))).astype(BF16)
    uu[rows_of(x), :] = (q * (a * sg)).astype(BF16)
    gather_start(aa, ag_s, ag_r)
    gather_start(uu, au_s, au_r)

    ct = 256 if cw % 256 == 0 else cw

    @pl.loop(0, NX)
    def _(step):
        k = turn(step)
        z_done(xs, xr, xss, xrs, k)
        ga = aa[rows_of(x), :]
        gu = uu[rows_of(x), :]

        @pl.loop(0, cw // ct)
        def _(n):
            c = pl.ds(pl.multiple_of(n * ct, ct), ct)
            xs[k, :, c] = (nt(ga, wg[k, c, :]) + nt(gu, wu[k, c, :])).astype(BF16)

        z_start(xs, ret, dss, drs, k)

    def ig_copies(k):
        return [
            pltpu.make_async_copy(
                up.at[k, :, pl.ds(h * cp, cp)], ig_ref.at[:, piece(k, h)], igs.at[k, h]
            )
            for h in range(ny)
        ]

    def combine():
        @pl.loop(0, NX)
        def _(step):
            k = turn(step)
            z_recv(xs, ret, dss, drs, k)
            up[k] = (up[k].astype(F32) + nn(selt[...], ret[k])).astype(BF16)

            @pl.when(is_last)
            def _():
                pipe_copy(k).start()

            for c in ig_copies(k):
                c.start()

    @pl.when(is_last)
    def _():
        combine()

    kh = wg.shape[2] // rows if wg.shape[2] % rows == 0 else 1

    def transposed(src, dst):
        for s in range(NX):
            for h in range(ny):
                dst[s // kh, h * cp : (h + 1) * cp, (s % kh) * rows : (s % kh + 1) * rows] = (
                    jnp.transpose(src[s, :, h * cp : (h + 1) * cp])
                )

    def product(lhs, rhs, h, n):
        c = pl.ds(pl.multiple_of(n * tile, tile), tile)
        r = pl.ds(pl.multiple_of(h * cp, cp), cp)
        acc = nn(lhs[0, r, :], rhs[0 : kh * rows, c])
        for m in range(1, NX // kh):
            acc += nn(lhs[m, r, :], rhs[m * kh * rows : (m + 1) * kh * rows, c])
        return acc

    def y_copy(t):
        return mesh_copy(wd.at[t, pl.ds(0, cp)], yrecv.at[t], ys.at[t], yr.at[t], y_peer)

    def for_peer(t, lhs, rhs):
        @pl.loop(0, ff // tile)
        def _(n):
            c = pl.ds(pl.multiple_of(n * tile, tile), tile)
            wd[t, 0:cp, c] = product(lhs, rhs, lax.rem(yh + 1, ny), n).astype(BF16)

        y_copy(t).start()

    def out_copy(t):
        out = (od_ref, og_ref, ou_ref)[t]
        return pltpu.make_async_copy(wd.at[t, pl.ds(cp, cp)], out, gos.at[t])

    def for_me(t, lhs, rhs):
        y_copy(t).wait()

        @pl.loop(0, ff // tile)
        def _(n):
            c = pl.ds(pl.multiple_of(n * tile, tile), tile)
            wd[t, cp : 2 * cp, c] = (
                product(lhs, rhs, yh, n) + yrecv[t, :, c].astype(F32)
            ).astype(BF16)

        out_copy(t).start()

    share_wait(dr, dsl, da_s, da_r, 1)
    transposed(dsl, wu)
    gather_wait(hh, h_s, h_r)
    for_peer(0, wu, hh)
    share_wait(xr, xsl, xa_s, xa_r, 0)
    transposed(xsl, wg)

    @pl.when(jnp.logical_not(is_last))
    def _():
        combine()

    gather_wait(aa, ag_s, ag_r)
    for_peer(1, wg, aa)
    gather_wait(uu, au_s, au_r)
    for_peer(2, wg, uu)
    for_me(0, wu, hh)
    for_me(1, wg, aa)
    for_me(2, wg, uu)

    @pl.loop(0, NX)
    def _(k):
        z_done(gs, dr, gss, grs, k)
        z_done(xs, ret, dss, drs, k)
        for c in ig_copies(k):
            c.wait()

        @pl.when(is_last)
        def _():
            pipe_copy(k).wait_send()

    for t in range(3):
        out_copy(t).wait()


def settle(*refs):
    count = (len(refs) - 2) // 3
    ins, outs, held = refs[:count], refs[count : 2 * count], refs[2 * count : 3 * count]
    got, put = refs[-2:]
    loads = [pltpu.make_async_copy(ins[i], held[i], got.at[i]) for i in range(count)]
    stores = [pltpu.make_async_copy(held[i], outs[i], put.at[i]) for i in range(count)]
    for c in loads:
        c.start()
    for load, store in zip(loads, stores):
        load.wait()
        store.start()
    for c in stores:
        c.wait()


def slots_of(routes, placement):
    micro, count, top = routes.shape
    experts = placement.shape[0]
    match = routes.reshape(micro, count * top)[:, :, None] == placement
    slot = jnp.sum(jnp.where(match, jnp.arange(experts, dtype=jnp.int32), 0), axis=2)
    order = jnp.arange(count * top)
    before = order[None, :] < order[:, None]
    same = slot[:, :, None] == slot[:, None, :]
    rank = jnp.sum((same & before).astype(jnp.int32), axis=2)
    place = (slot * micro + jnp.arange(micro, dtype=jnp.int32)[:, None]) * CAP + rank
    return place.reshape(micro * count, top)


def local(
    activations, cotangent, routes, route_weights, placement, gate_weight, up_weight, down_weight
):
    ne = lax.axis_size("expert")
    ny = lax.axis_size("dp") // NX
    _, micro, count, d = activations.shape
    tokens = micro * count
    ff = gate_weight.shape[3]
    rows = ne * micro * CAP
    cw = d // NX
    cp = cw // ny
    place = slots_of(routes[0], placement[0])
    vm = functools.partial(pl.BlockSpec, memory_space=pltpu.VMEM)
    hbm = functools.partial(pl.BlockSpec, memory_space=pl.ANY)
    dma = pltpu.SemaphoreType.DMA
    wide = pltpu.VMEM((NX, rows, cw), BF16)
    tall = pltpu.VMEM((NX * rows, ff), BF16)
    weight = pltpu.VMEM((NX, cw, ff), BF16)
    acc = pltpu.VMEM((rows, ff), F32)
    outs = pl.pallas_call(
        mega,
        out_shape=(
            jax.ShapeDtypeStruct((tokens, d), BF16),
            jax.ShapeDtypeStruct((cp, ff), BF16),
            jax.ShapeDtypeStruct((cp, ff), BF16),
            jax.ShapeDtypeStruct((cp, ff), BF16),
        ),
        in_specs=[vm()] * 5 + [hbm()] * 3,
        out_specs=(hbm(),) * 4,
        scratch_shapes=[
            weight, weight, weight,
            wide, wide, wide, wide, wide,
            pltpu.VMEM((NX, tokens, cw), BF16),
            wide, wide,
            tall, tall, tall,
            pltpu.VMEM((3, cp, ff), BF16),
            pltpu.VMEM((rows, tokens), BF16),
            pltpu.VMEM((tokens, rows), BF16),
            pltpu.VMEM((rows, 128), F32),
            acc, acc, acc,
            dma((3, NX, ny)),
            dma((NX, ne)), dma((NX, ne)), dma((NX, ne)), dma((NX, ne)),
            dma((NX, ne)), dma((NX, ne)),
            dma((2,)),
            dma((NX,)), dma((NX,)),
            dma((NX,)), dma((NX,)), dma((NX,)), dma((NX,)),
            dma((NX,)), dma((NX,)), dma((NX,)), dma((NX,)), dma((NX,)), dma((NX,)),
            dma((3,)), dma((3,)), dma((NX, ny)), dma((3,)),
        ],
        compiler_params=pltpu.CompilerParams(
            collective_id=0, has_side_effects=True, vmem_limit_bytes=63 * 2**20
        ),
        cost_estimate=pl.CostEstimate(
            flops=20 * 10**9, bytes_accessed=24 * 10**6, transcendentals=10**6
        ),
    )(
        activations.reshape(tokens, d),
        cotangent.reshape(tokens, d),
        place.T,
        place,
        route_weights.reshape(tokens, -1).T,
        gate_weight[0, 0],
        up_weight[0, 0],
        down_weight[0, 0],
    )
    outs = pl.pallas_call(
        settle,
        out_shape=tuple(jax.ShapeDtypeStruct(o.shape, o.dtype) for o in outs),
        in_specs=[hbm()] * 4,
        out_specs=(hbm(),) * 4,
        scratch_shapes=[pltpu.VMEM(o.shape, o.dtype) for o in outs] + [dma((4,)), dma((4,))],
    )(*outs)
    return (
        outs[0].reshape(1, micro, count, d),
        outs[1][None, None],
        outs[2][None, None],
        outs[3][None, None],
    )


def solution(mesh):
    blocks = ("expert", "dp")
    placed = (
        P("pipe", None, blocks, None),
        P(None, blocks, None),
        P("pipe", None, blocks, None),
        P("pipe", None, blocks, None),
        P("pipe", None),
        P("pipe", "expert", None, None),
        P("pipe", "expert", None, None),
        P("pipe", "expert", None, None),
    )
    return jax.shard_map(
        local,
        mesh=mesh,
        in_specs=placed,
        out_specs=(
            P("pipe", None, blocks, None),
            P("pipe", "expert", "dp", None),
            P("pipe", "expert", "dp", None),
            P("pipe", "expert", "dp", None),
        ),
        check_vma=False,
    )
```

```python
import functools

import jax
import jax.numpy as jnp
from jax import lax
from jax.experimental import pallas as pl
from jax.experimental.pallas import tpu as pltpu
from jax.sharding import PartitionSpec as P

CAP = 24
NX = 4
F32 = jnp.float32
BF16 = jnp.bfloat16


def nt(left, right):
    return lax.dot_general(left, right, (((1,), (1,)), ((), ())), preferred_element_type=F32)


def nn(left, right):
    return jnp.dot(left, right, preferred_element_type=F32)


def mega(
    micro, x_ref, cot_ref, routes_ref, rw_ref, place_ref, wg_hbm, wu_hbm, wd_hbm,
    ig_ref, og_ref, ou_ref, od_ref,
    wg, wu, wd, xs, gs, xr, dr, ret, up, xsl, dsl, hh, aa, uu, yrecv,
    sel, selt, scale, a_acc, u_acc, q_acc,
    wsem, xss, xrs, gss, grs, dss, drs, lsem, pss, prs,
    xa_s, xa_r, da_s, da_r, h_s, h_r, ag_s, ag_r, au_s, au_r, ys, yr, igs, gos,
):
    p = lax.axis_index("pipe")
    me = lax.axis_index("expert")
    j = lax.axis_index("dp")
    ne = lax.axis_size("expert")
    ndp = lax.axis_size("dp")
    ny = ndp // NX
    x = lax.rem(j, NX)
    yh = j // NX
    last = lax.axis_size("pipe") - 1
    tokens, d = x_ref.shape
    rows = sel.shape[0]
    blk = rows // ne
    ff = wg.shape[2]
    cw = d // NX
    cp = cw // ny
    is_last = p == last

    def at_z(e):
        return (p, e, j)

    def at_x(k):
        return (p, me, yh * NX + k)

    def mesh_copy(src, dst, s, r, dev):
        return pltpu.make_async_remote_copy(
            src_ref=src, dst_ref=dst, send_sem=s, recv_sem=r,
            device_id=dev, device_id_type=pl.DeviceIdType.MESH,
        )

    y_peer = (p, me, lax.rem(yh + 1, ny) * NX + x)
    p_peer = (last - p, me, j)

    def w_copies(t, k):
        src, dst = ((wg_hbm, wg), (wu_hbm, wu), (wd_hbm, wd))[t]
        return [
            pltpu.make_async_copy(
                src.at[pl.ds(h * (d // ny) + k * cp, cp)],
                dst.at[k, pl.ds(h * cp, cp)],
                wsem.at[t, k, h],
            )
            for h in range(ny)
        ]

    for t in range(3):
        for k in range(NX):
            for c in w_copies(t, k):
                c.start()

    barrier = pltpu.get_barrier_semaphore()
    peers = [at_z(lax.rem(me + o, ne)) for o in range(1, ne)]
    peers += [at_x(lax.rem(x + o, NX)) for o in range(1, NX)]
    peers += [y_peer, p_peer]
    for dev in peers:
        pl.semaphore_signal(barrier, inc=1, device_id=dev, device_id_type=pl.DeviceIdType.MESH)

    square = (tokens, tokens)
    t_row = lax.broadcasted_iota(jnp.int32, square, 0)
    t_col = lax.broadcasted_iota(jnp.int32, square, 1)
    count = tokens // micro
    before = (t_col < t_row) & (t_col // count == t_row // count)
    ids = routes_ref[...]
    slots = jnp.zeros(ids.shape, jnp.int32)
    for s in range(ne):
        slots = jnp.where(ids == place_ref[0, s], s, slots)
    slots = slots.astype(F32)
    by_row = [jnp.broadcast_to(slots[:, k : k + 1], square) for k in range(2)]
    by_col = [jnp.transpose(v) for v in by_row]
    micro_of = (lax.broadcasted_iota(jnp.int32, (tokens, 1), 0) // count).astype(F32)
    places = []
    for k in range(2):
        same = jnp.where(by_col[0] == by_row[k], 1.0, 0.0) + jnp.where(
            by_col[1] == by_row[k], 1.0, 0.0
        )
        rank = jnp.sum(jnp.where(before, same, 0.0), axis=1, keepdims=True)
        places.append(slots[:, k : k + 1] * blk + micro_of * CAP + rank)

    def as_row(column):
        return jnp.transpose(jnp.broadcast_to(column, square))[0:1, :]

    r_iota = lax.broadcasted_iota(jnp.int32, (rows, tokens), 0).astype(F32)
    hits = [r_iota == as_row(v) for v in places]
    sel[...] = jnp.where(hits[0] | hits[1], 1.0, 0.0).astype(BF16)
    weight = sum(
        jnp.where(hits[k], as_row(rw_ref[:, k : k + 1]), 0.0) for k in range(2)
    )
    scale[...] = jnp.broadcast_to(jnp.sum(weight, axis=1, keepdims=True), scale.shape)
    c_iota = lax.broadcasted_iota(jnp.int32, (tokens, rows), 1).astype(F32)
    selt[...] = jnp.where((c_iota == places[0]) | (c_iota == places[1]), 1.0, 0.0).astype(BF16)

    pl.semaphore_wait(barrier, len(peers))

    def my_rows(e):
        return pl.ds(pl.multiple_of(e * blk, 16), blk)

    def z_sends(stage, land, ss, rs, k):
        out = []
        for o in range(1, ne):
            e = lax.rem(me + o, ne)
            out.append(
                mesh_copy(
                    stage.at[k, my_rows(e)], land.at[k, my_rows(me)],
                    ss.at[k, o], rs.at[k, o], at_z(e),
                )
            )
        return out

    def z_own(stage, land, ss, k):
        return pltpu.make_async_copy(
            stage.at[k, my_rows(me)], land.at[k, my_rows(me)], ss.at[k, 0]
        )

    def z_start(stage, land, ss, rs, k):
        for c in z_sends(stage, land, ss, rs, k):
            c.start()
        z_own(stage, land, ss, k).start()

    def z_recv(stage, land, ss, rs, k):
        for o in range(1, ne):
            e = lax.rem(me + ne - o, ne)
            mesh_copy(
                stage.at[k, my_rows(e)], land.at[k, my_rows(e)],
                ss.at[k, o], rs.at[k, o], at_z(e),
            ).wait_recv()
        z_own(stage, land, ss, k).wait()

    def z_done(stage, land, ss, rs, k):
        for c in z_sends(stage, land, ss, rs, k):
            c.wait_send()

    def piece(k, h):
        return pl.ds(pl.multiple_of(h * (d // ny) + k * cp, cp), cp)

    def chunk_of(ref, k):
        return jnp.concatenate([ref[:, piece(k, h)] for h in range(ny)], axis=1)

    def send_scaled(k):
        picked = nn(sel[...], up[k])
        gs[k] = (scale[:, 0:1] * picked).astype(BF16)
        z_start(gs, dr, gss, grs, k)

    def turn(step):
        return lax.rem(x + step, NX)

    @pl.loop(0, NX)
    def _(step):
        k = turn(step)
        xs[k] = nn(sel[...], chunk_of(x_ref, k)).astype(BF16)
        z_start(xs, xr, xss, xrs, k)

        @pl.when(is_last)
        def _():
            up[k] = chunk_of(cot_ref, k)
            send_scaled(k)

    def share_copy(src, dst, ss, rs, k):
        return mesh_copy(src.at[k], dst.at[x], ss.at[k], rs.at[x], at_x(k))

    def share_local(src, dst, k, n):
        return pltpu.make_async_copy(src.at[k], dst.at[k], lsem.at[n])

    def share_start(src, dst, ss, rs, k, n):
        @pl.when(k != x)
        def _():
            share_copy(src, dst, ss, rs, k).start()

        @pl.when(k == x)
        def _():
            share_local(src, dst, k, n).start()

    def share_wait(src, dst, ss, rs, n):
        for o in range(1, NX):
            k = lax.rem(x + o, NX)
            share_copy(src, dst, ss, rs, k).wait_send()
            mesh_copy(src.at[k], dst.at[k], ss.at[k], rs.at[k], at_x(k)).wait_recv()
        share_local(src, dst, x, n).wait()

    def rows_of(s):
        return pl.ds(pl.multiple_of(s * rows, 16), rows)

    def gather(buf, ss, rs):
        return [
            mesh_copy(
                buf.at[rows_of(x)], buf.at[rows_of(x)], ss.at[o], rs.at[o],
                at_x(lax.rem(x + o, NX)),
            )
            for o in range(1, NX)
        ]

    def gather_start(buf, ss, rs):
        for c in gather(buf, ss, rs):
            c.start()

    def gather_wait(buf, ss, rs):
        for o, c in zip(range(1, NX), gather(buf, ss, rs)):
            c.wait_send()
            s = lax.rem(x + NX - o, NX)
            mesh_copy(
                buf.at[rows_of(s)], buf.at[rows_of(s)], ss.at[o], rs.at[o], at_x(s)
            ).wait_recv()

    tile = 256

    pieces = ff // tile
    half = rows // 2
    right, left = lax.rem(x + 1, NX), lax.rem(x + NX - 1, NX)
    across = lax.rem(x + 2, NX)

    def ring_copy(buf, ss, rs, n, way, owner, first, count, to):
        part = buf.at[
            pl.ds(pl.multiple_of(owner * rows + first, 16), count), pl.ds(n * tile, tile)
        ]
        return mesh_copy(part, part, ss.at[n, way], rs.at[n, way], at_x(to))

    def ring_start(buf, ss, rs, n):
        ring_copy(buf, ss, rs, n, 0, x, 0, rows, right).start()
        ring_copy(buf, ss, rs, n, 1, x, 0, rows, left).start()

    def ring_pass(buf, ss, rs, n):
        ring_copy(buf, ss, rs, n, 0, left, 0, rows, right).wait_recv()
        ring_copy(buf, ss, rs, n, 2, left, 0, half, right).start()
        ring_copy(buf, ss, rs, n, 1, right, 0, rows, left).wait_recv()
        ring_copy(buf, ss, rs, n, 3, right, half, half, left).start()

    def ring_wait(buf, ss, rs, n):
        ring_copy(buf, ss, rs, n, 2, across, 0, half, right).wait_recv()
        ring_copy(buf, ss, rs, n, 3, across, half, half, left).wait_recv()

    def ring_done(buf, ss, rs, n):
        ring_copy(buf, ss, rs, n, 0, x, 0, rows, right).wait_send()
        ring_copy(buf, ss, rs, n, 1, x, 0, rows, left).wait_send()
        ring_copy(buf, ss, rs, n, 2, left, 0, half, right).wait_send()
        ring_copy(buf, ss, rs, n, 3, right, half, half, left).wait_send()

    a_acc[...] = jnp.zeros_like(a_acc)
    u_acc[...] = jnp.zeros_like(u_acc)
    q_acc[...] = jnp.zeros_like(q_acc)

    def wait_w(t, k):
        for c in w_copies(t, k):
            c.wait()

    @pl.loop(0, NX)
    def _(step):
        k = turn(step)
        z_recv(xs, xr, xss, xrs, k)
        share_start(xr, xsl, xa_s, xa_r, k, 0)
        wait_w(0, k)
        wait_w(1, k)

        @pl.loop(0, ff // tile)
        def _(n):
            c = pl.ds(pl.multiple_of(n * tile, tile), tile)
            a_acc[:, c] += nn(xr[k], wg[k, :, c])
            u_acc[:, c] += nn(xr[k], wu[k, :, c])

    a = a_acc[...]
    hh[rows_of(x), :] = (a * jax.nn.sigmoid(a) * u_acc[...]).astype(BF16)
    gather_start(hh, h_s, h_r)

    def pipe_copy(k):
        return mesh_copy(up.at[k], up.at[k], pss.at[k], prs.at[k], p_peer)

    def take_dr(k):
        z_recv(gs, dr, gss, grs, k)
        share_start(dr, dsl, da_s, da_r, k, 1)
        wait_w(2, k)

        @pl.loop(0, ff // tile)
        def _(n):
            c = pl.ds(pl.multiple_of(n * tile, tile), tile)
            q_acc[:, c] += nn(dr[k], wd[k, :, c])

    @pl.loop(0, NX + 1)
    def _(step):
        @pl.when(jnp.logical_not(is_last) & (step < NX))
        def _():
            pipe_copy(turn(step)).wait_recv()
            send_scaled(turn(step))

        @pl.when(step > 0)
        def _():
            take_dr(turn(step + NX - 1))

    a = a_acc[...]
    sg = jax.nn.sigmoid(a)
    q = q_acc[...]
    aa[rows_of(x), :] = (q * u_acc[...] * sg * (1.0 + a * (1.0 - sg))).astype(BF16)
    uu[rows_of(x), :] = (q * (a * sg)).astype(BF16)
    for n in range(pieces):
        ring_start(aa, ag_s, ag_r, n)
    for n in range(pieces):
        ring_start(uu, au_s, au_r, n)

    ct = 256 if cw % 256 == 0 else cw

    @pl.loop(0, NX)
    def _(step):
        k = turn(step)
        z_done(xs, xr, xss, xrs, k)
        ga = aa[rows_of(x), :]
        gu = uu[rows_of(x), :]

        @pl.loop(0, cw // ct)
        def _(n):
            c = pl.ds(pl.multiple_of(n * ct, ct), ct)
            xs[k, :, c] = (nt(ga, wg[k, c, :]) + nt(gu, wu[k, c, :])).astype(BF16)

        z_start(xs, ret, dss, drs, k)

    def ig_copies(k):
        return [
            pltpu.make_async_copy(
                up.at[k, :, pl.ds(h * cp, cp)], ig_ref.at[:, piece(k, h)], igs.at[k, h]
            )
            for h in range(ny)
        ]

    def combine():
        @pl.loop(0, NX)
        def _(step):
            k = turn(step)
            z_recv(xs, ret, dss, drs, k)
            up[k] = (up[k].astype(F32) + nn(selt[...], ret[k])).astype(BF16)

            @pl.when(is_last)
            def _():
                pipe_copy(k).start()

            for c in ig_copies(k):
                c.start()

    @pl.when(is_last)
    def _():
        combine()

    kh = wg.shape[2] // rows if wg.shape[2] % rows == 0 else 1

    def transposed(src, dst):
        for s in range(NX):
            for h in range(ny):
                dst[s // kh, h * cp : (h + 1) * cp, (s % kh) * rows : (s % kh + 1) * rows] = (
                    jnp.transpose(src[s, :, h * cp : (h + 1) * cp])
                )

    def columns(n):
        return pl.ds(n * tile, tile)

    def product(lhs, rhs, h, n):
        c = columns(n)
        r = pl.ds(pl.multiple_of(h * cp, cp), cp)
        acc = nn(lhs[0, r, :], rhs[0 : kh * rows, c])
        for m in range(1, NX // kh):
            acc += nn(lhs[m, r, :], rhs[m * kh * rows : (m + 1) * kh * rows, c])
        return acc

    def y_copy(t, n):
        return mesh_copy(
            wd.at[t, pl.ds(0, cp), columns(n)], yrecv.at[t, :, columns(n)],
            ys.at[t, n], yr.at[t, n], y_peer,
        )

    def for_peer(t, lhs, rhs, n):
        wd[t, 0:cp, columns(n)] = product(lhs, rhs, lax.rem(yh + 1, ny), n).astype(BF16)
        y_copy(t, n).start()

    def out_copy(t, n):
        out = (od_ref, og_ref, ou_ref)[t]
        return pltpu.make_async_copy(
            wd.at[t, pl.ds(cp, cp), columns(n)], out.at[:, columns(n)], gos.at[t, n]
        )

    def for_me(t, lhs, rhs, n):
        mine = product(lhs, rhs, yh, n)
        y_copy(t, n).wait()
        wd[t, cp : 2 * cp, columns(n)] = (
            mine + yrecv[t, :, columns(n)].astype(F32)
        ).astype(BF16)
        out_copy(t, n).start()

    ring = [(aa, ag_s, ag_r, n) for n in range(pieces)]
    ring += [(uu, au_s, au_r, n) for n in range(pieces)]
    ring_pass(*ring[0])
    share_wait(dr, dsl, da_s, da_r, 1)
    transposed(dsl, wu)
    ring_pass(*ring[1])
    gather_wait(hh, h_s, h_r)
    for n in range(pieces):
        for_peer(0, wu, hh, n)
    ring_pass(*ring[2])
    share_wait(xr, xsl, xa_s, xa_r, 0)
    transposed(xsl, wg)
    for i in range(len(ring)):
        if i + 3 < len(ring):
            ring_pass(*ring[i + 3])
        ring_wait(*ring[i])
        for_peer(1 + i // pieces, wg, ring[i][0], i % pieces)

    @pl.when(jnp.logical_not(is_last))
    def _():
        combine()

    for n in range(pieces):
        for_me(0, wu, hh, n)
    for i in range(len(ring)):
        for_me(1 + i // pieces, wg, ring[i][0], i % pieces)
    for args in ring:
        ring_done(*args)

    @pl.loop(0, NX)
    def _(k):
        z_done(gs, dr, gss, grs, k)
        z_done(xs, ret, dss, drs, k)
        for c in ig_copies(k):
            c.wait()

        @pl.when(is_last)
        def _():
            pipe_copy(k).wait_send()

    for t in range(3):
        for n in range(pieces):
            out_copy(t, n).wait()


def settle(*refs):
    count = (len(refs) - 2) // 3
    ins, outs, held = refs[:count], refs[count : 2 * count], refs[2 * count : 3 * count]
    got, put = refs[-2:]
    loads = [pltpu.make_async_copy(ins[i], held[i], got.at[i]) for i in range(count)]
    stores = [pltpu.make_async_copy(held[i], outs[i], put.at[i]) for i in range(count)]
    for c in loads:
        c.start()
    for load, store in zip(loads, stores):
        load.wait()
        store.start()
    for c in stores:
        c.wait()


def local(
    activations, cotangent, routes, route_weights, placement, gate_weight, up_weight, down_weight
):
    ne = lax.axis_size("expert")
    ny = lax.axis_size("dp") // NX
    _, micro, count, d = activations.shape
    tokens = micro * count
    ff = gate_weight.shape[3]
    rows = ne * micro * CAP
    cw = d // NX
    cp = cw // ny
    vm = functools.partial(pl.BlockSpec, memory_space=pltpu.VMEM)
    hbm = functools.partial(pl.BlockSpec, memory_space=pl.ANY)
    dma = pltpu.SemaphoreType.DMA
    wide = pltpu.VMEM((NX, rows, cw), BF16)
    tall = pltpu.VMEM((NX * rows, ff), BF16)
    weight = pltpu.VMEM((NX, cw, ff), BF16)
    acc = pltpu.VMEM((rows, ff), F32)
    np_ = ff // 256
    outs = pl.pallas_call(
        functools.partial(mega, micro),
        out_shape=(
            jax.ShapeDtypeStruct((tokens, d), BF16),
            jax.ShapeDtypeStruct((cp, ff), BF16),
            jax.ShapeDtypeStruct((cp, ff), BF16),
            jax.ShapeDtypeStruct((cp, ff), BF16),
        ),
        in_specs=[vm()] * 4 + [pl.BlockSpec(memory_space=pltpu.SMEM)] + [hbm()] * 3,
        out_specs=(hbm(),) * 4,
        scratch_shapes=[
            weight, weight, weight,
            wide, wide, wide, wide, wide,
            pltpu.VMEM((NX, tokens, cw), BF16),
            wide, wide,
            tall, tall, tall,
            pltpu.VMEM((3, cp, ff), BF16),
            pltpu.VMEM((rows, tokens), BF16),
            pltpu.VMEM((tokens, rows), BF16),
            pltpu.VMEM((rows, 128), F32),
            acc, acc, acc,
            dma((3, NX, ny)),
            dma((NX, ne)), dma((NX, ne)), dma((NX, ne)), dma((NX, ne)),
            dma((NX, ne)), dma((NX, ne)),
            dma((2,)),
            dma((NX,)), dma((NX,)),
            dma((NX,)), dma((NX,)), dma((NX,)), dma((NX,)),
            dma((NX,)), dma((NX,)), dma((np_, 4)), dma((np_, 4)), dma((np_, 4)), dma((np_, 4)),
            dma((3, np_)), dma((3, np_)), dma((NX, ny)), dma((3, np_)),
        ],
        compiler_params=pltpu.CompilerParams(
            collective_id=0, has_side_effects=True, vmem_limit_bytes=63 * 2**20
        ),
        cost_estimate=pl.CostEstimate(
            flops=20 * 10**9, bytes_accessed=24 * 10**6, transcendentals=10**6
        ),
    )(
        activations.reshape(tokens, d),
        cotangent.reshape(tokens, d),
        routes.reshape(tokens, -1),
        route_weights.reshape(tokens, -1),
        placement,
        gate_weight[0, 0],
        up_weight[0, 0],
        down_weight[0, 0],
    )
    outs = pl.pallas_call(
        settle,
        out_shape=tuple(jax.ShapeDtypeStruct(o.shape, o.dtype) for o in outs),
        in_specs=[hbm()] * 4,
        out_specs=(hbm(),) * 4,
        scratch_shapes=[pltpu.VMEM(o.shape, o.dtype) for o in outs] + [dma((4,)), dma((4,))],
    )(*outs)
    return (
        outs[0].reshape(1, micro, count, d),
        outs[1][None, None],
        outs[2][None, None],
        outs[3][None, None],
    )


def solution(mesh):
    blocks = ("expert", "dp")
    placed = (
        P("pipe", None, blocks, None),
        P(None, blocks, None),
        P("pipe", None, blocks, None),
        P("pipe", None, blocks, None),
        P("pipe", None),
        P("pipe", "expert", None, None),
        P("pipe", "expert", None, None),
        P("pipe", "expert", None, None),
    )
    return jax.shard_map(
        local,
        mesh=mesh,
        in_specs=placed,
        out_specs=(
            P("pipe", None, blocks, None),
            P("pipe", "expert", "dp", None),
            P("pipe", "expert", "dp", None),
            P("pipe", "expert", "dp", None),
        ),
        check_vma=False,
    )
```

```python
import functools

import jax
import jax.numpy as jnp
from jax import lax
from jax.experimental import pallas as pl
from jax.experimental.pallas import tpu as pltpu
from jax.sharding import PartitionSpec as P

CAP = 24
RELAYED = 4
NX = 4
F32 = jnp.float32
BF16 = jnp.bfloat16


def nt(left, right):
    return lax.dot_general(left, right, (((1,), (1,)), ((), ())), preferred_element_type=F32)


def nn(left, right):
    return jnp.dot(left, right, preferred_element_type=F32)


def mega(
    micro, x_ref, cot_ref, routes_ref, rw_ref, place_ref, wg_hbm, wu_hbm, wd_hbm,
    ig_ref, og_ref, ou_ref, od_ref,
    wg, wu, wd, xs, gs, xr, dr, ret, up, xsl, dsl, hh, aa, uu, yrecv,
    sel, selt, scale, rel, tab, sel1, scale1, a_acc, u_acc, q_acc,
    wsem, xss, xrs, gss, grs, dss, drs, lsem, pss, prs,
    xa_s, xa_r, da_s, da_r, h_s, h_r, ag_s, ag_r, au_s, au_r, ys, yr, igs, gos,
    rls, rlr, fws, fwr, tbs, tbr,
):
    p = lax.axis_index("pipe")
    me = lax.axis_index("expert")
    j = lax.axis_index("dp")
    ne = lax.axis_size("expert")
    ndp = lax.axis_size("dp")
    ny = ndp // NX
    x = lax.rem(j, NX)
    yh = j // NX
    last = lax.axis_size("pipe") - 1
    tokens, d = x_ref.shape
    rows = sel.shape[0]
    blk = rows // ne
    ff = wg.shape[2]
    nc = ndp
    cp = d // nc
    is_last = p == last

    def at_z(e):
        return (p, e, j)

    def at_x(k):
        return (p, me, yh * NX + k)

    def mesh_copy(src, dst, s, r, dev):
        return pltpu.make_async_remote_copy(
            src_ref=src, dst_ref=dst, send_sem=s, recv_sem=r,
            device_id=dev, device_id_type=pl.DeviceIdType.MESH,
        )

    def chunk(k):
        return pl.ds(pl.multiple_of(k * cp, cp), cp)

    y_peer = (p, me, lax.rem(yh + 1, ny) * NX + x)
    p_peer = (last - p, me, j)

    def w_copy(t, k):
        src, dst = ((wg_hbm, wg), (wu_hbm, wu), (wd_hbm, wd))[t]
        return pltpu.make_async_copy(src.at[chunk(k)], dst.at[k], wsem.at[t, k])

    for t in range(3):
        for k in range(nc):
            w_copy(t, k).start()

    barrier = pltpu.get_barrier_semaphore()
    peers = [at_z(lax.rem(me + o, ne)) for o in range(1, ne)]
    peers += [at_x(lax.rem(x + o, NX)) for o in range(1, NX)]
    peers += [y_peer, p_peer]
    for dev in peers:
        pl.semaphore_signal(barrier, inc=1, device_id=dev, device_id_type=pl.DeviceIdType.MESH)

    square = (tokens, tokens)
    t_row = lax.broadcasted_iota(jnp.int32, square, 0)
    t_col = lax.broadcasted_iota(jnp.int32, square, 1)
    count = tokens // micro
    before = (t_col < t_row) & (t_col // count == t_row // count)
    micro_of = (lax.broadcasted_iota(jnp.int32, (tokens, 1), 0) // count).astype(F32)

    def as_row(column):
        return jnp.transpose(jnp.broadcast_to(column, square))[0:1, :]

    def tables(slots, weights, sel, scale):
        by_row = [jnp.broadcast_to(slots[:, k : k + 1], square) for k in range(2)]
        by_col = [jnp.transpose(v) for v in by_row]
        places = []
        for k in range(2):
            same = jnp.where(by_col[0] == by_row[k], 1.0, 0.0) + jnp.where(
                by_col[1] == by_row[k], 1.0, 0.0
            )
            rank = jnp.sum(jnp.where(before, same, 0.0), axis=1, keepdims=True)
            places.append(slots[:, k : k + 1] * blk + micro_of * CAP + rank)
        r_iota = lax.broadcasted_iota(jnp.int32, (rows, tokens), 0).astype(F32)
        hits = [r_iota == as_row(v) for v in places]
        sel[...] = jnp.where(hits[0] | hits[1], 1.0, 0.0).astype(BF16)
        weight = sum(jnp.where(hits[k], as_row(weights[:, k : k + 1]), 0.0) for k in range(2))
        scale[...] = jnp.broadcast_to(jnp.sum(weight, axis=1, keepdims=True), scale.shape)
        return places

    ids = routes_ref[...]
    slots = jnp.zeros(ids.shape, jnp.int32)
    for s in range(ne):
        slots = jnp.where(ids == place_ref[0, s], s, slots)
    slots = slots.astype(F32)

    @pl.when(is_last)
    def _():
        packed = jnp.zeros(tab.shape, F32)
        lane = lax.broadcasted_iota(jnp.int32, tab.shape, 1)
        for k in range(2):
            packed = jnp.where(lane == k, slots[:, k : k + 1], packed)
            packed = jnp.where(lane == 2 + k, rw_ref[:, k : k + 1], packed)
        tab[...] = packed

    tab_copy = mesh_copy(tab, tab, tbs.at[0], tbr.at[0], p_peer)

    pl.semaphore_wait(barrier, len(peers))

    @pl.when(is_last)
    def _():
        tab_copy.start()

    places = tables(slots, rw_ref[...], sel, scale)
    c_iota = lax.broadcasted_iota(jnp.int32, (tokens, rows), 1).astype(F32)
    selt[...] = jnp.where((c_iota == places[0]) | (c_iota == places[1]), 1.0, 0.0).astype(BF16)

    def my_rows(e):
        return pl.ds(pl.multiple_of(e * blk, 16), blk)

    def z_sends(stage, land, ss, rs, k):
        out = []
        for o in range(1, ne):
            e = lax.rem(me + o, ne)
            out.append(
                mesh_copy(
                    stage.at[k, my_rows(e)], land.at[k, my_rows(me)],
                    ss.at[k, o], rs.at[k, o], at_z(e),
                )
            )
        return out

    def z_own(stage, land, ss, k):
        return pltpu.make_async_copy(
            stage.at[k, my_rows(me)], land.at[k, my_rows(me)], ss.at[k, 0]
        )

    def z_start(stage, land, ss, rs, k):
        for c in z_sends(stage, land, ss, rs, k):
            c.start()
        z_own(stage, land, ss, k).start()

    def z_recv(stage, land, ss, rs, k):
        for o in range(1, ne):
            e = lax.rem(me + ne - o, ne)
            mesh_copy(
                stage.at[k, my_rows(e)], land.at[k, my_rows(e)],
                ss.at[k, o], rs.at[k, o], at_z(e),
            ).wait_recv()
        z_own(stage, land, ss, k).wait()

    def z_done(stage, land, ss, rs, k):
        for c in z_sends(stage, land, ss, rs, k):
            c.wait_send()

    def send_scaled(k):
        picked = nn(sel[...], up[k])
        gs[k] = (scale[:, 0:1] * picked).astype(BF16)
        z_start(gs, dr, gss, grs, k)

    def turn(step):
        own = step // (2 * NX - 2)
        r = lax.rem(step, 3)
        o = (1 - own) * (1 + 2 * r - 3 * (r // 2))
        h = (1 - own) * (step // 3) + own * (step - (2 * NX - 2))
        return h * NX + lax.rem(x + o, NX)

    direct = nc - RELAYED

    def relay_copy(m, o):
        e = lax.rem(me + o, ne)
        return mesh_copy(
            gs.at[turn(direct + m), my_rows(e)], rel.at[m, my_rows(me)],
            rls.at[m, o], rlr.at[m, o], at_z(e),
        )

    def relay_own(m):
        return pltpu.make_async_copy(
            gs.at[turn(direct + m), my_rows(me)], rel.at[m, my_rows(me)], rls.at[m, 0]
        )

    def hand_up(m):
        return mesh_copy(rel.at[m], dr.at[turn(direct + m)], fws.at[m], fwr.at[m], p_peer)

    def send_inputs(step):
        k = turn(step)
        xs[k] = nn(sel[...], x_ref[:, chunk(k)]).astype(BF16)
        z_start(xs, xr, xss, xrs, k)

        @pl.when(is_last)
        def _():
            up[k] = cot_ref[:, chunk(k)]

        @pl.when(is_last & (step < direct))
        def _():
            send_scaled(k)

    @pl.loop(0, 2)
    def _(step):
        send_inputs(step)

    @pl.when(jnp.logical_not(is_last))
    def _():
        tab_copy.wait_recv()
        tables(tab[:, 0:2], tab[:, 2:4], sel1, scale1)

        @pl.loop(0, RELAYED)
        def _(m):
            k = turn(direct + m)
            picked = nn(sel1[...], cot_ref[:, chunk(k)])
            gs[k] = (scale1[:, 0:1] * picked).astype(BF16)
            for o in range(1, ne):
                relay_copy(m, o).start()
            relay_own(m).start()

    @pl.loop(2, nc)
    def _(step):
        send_inputs(step)

    @pl.when(jnp.logical_not(is_last))
    def _():
        @pl.loop(0, RELAYED)
        def _(m):
            for o in range(1, ne):
                e = lax.rem(me + ne - o, ne)
                mesh_copy(
                    gs.at[turn(direct + m), my_rows(e)], rel.at[m, my_rows(e)],
                    rls.at[m, o], rlr.at[m, o], at_z(e),
                ).wait_recv()
            relay_own(m).wait()
            hand_up(m).start()
            for o in range(1, ne):
                relay_copy(m, o).wait_send()

    def share_copy(src, dst, ss, rs, k):
        return mesh_copy(
            src.at[k], dst.at[x, k // NX], ss.at[k], rs.at[x, k // NX], at_x(lax.rem(k, NX))
        )

    def share_local(src, dst, k, n):
        return pltpu.make_async_copy(src.at[k], dst.at[x, k // NX], lsem.at[n, k // NX])

    def share_start(src, dst, ss, rs, k, n):
        @pl.when(lax.rem(k, NX) != x)
        def _():
            share_copy(src, dst, ss, rs, k).start()

        @pl.when(lax.rem(k, NX) == x)
        def _():
            share_local(src, dst, k, n).start()

    def share_wait(src, dst, ss, rs, n):
        for h in range(ny):
            for o in range(1, NX):
                s = lax.rem(x + o, NX)
                k = h * NX + s
                share_copy(src, dst, ss, rs, k).wait_send()
                mesh_copy(src.at[k], dst.at[s, h], ss.at[k], rs.at[s, h], at_x(s)).wait_recv()
            share_local(src, dst, h * NX + x, n).wait()

    def rows_of(s):
        return pl.ds(pl.multiple_of(s * rows, 16), rows)

    def gather(buf, ss, rs):
        return [
            mesh_copy(
                buf.at[rows_of(x)], buf.at[rows_of(x)], ss.at[o], rs.at[o],
                at_x(lax.rem(x + o, NX)),
            )
            for o in range(1, NX)
        ]

    def gather_start(buf, ss, rs):
        for c in gather(buf, ss, rs):
            c.start()

    def gather_wait(buf, ss, rs):
        for o, c in zip(range(1, NX), gather(buf, ss, rs)):
            c.wait_send()
            s = lax.rem(x + NX - o, NX)
            mesh_copy(
                buf.at[rows_of(s)], buf.at[rows_of(s)], ss.at[o], rs.at[o], at_x(s)
            ).wait_recv()

    tile = 256

    pieces = ff // tile
    half = rows // 2
    right, left = lax.rem(x + 1, NX), lax.rem(x + NX - 1, NX)
    across = lax.rem(x + 2, NX)

    def ring_copy(buf, ss, rs, n, way, owner, first, count, to):
        part = buf.at[
            pl.ds(pl.multiple_of(owner * rows + first, 16), count), pl.ds(n * tile, tile)
        ]
        return mesh_copy(part, part, ss.at[n, way], rs.at[n, way], at_x(to))

    def ring_start(buf, ss, rs, n):
        ring_copy(buf, ss, rs, n, 0, x, 0, rows, right).start()
        ring_copy(buf, ss, rs, n, 1, x, 0, rows, left).start()

    def ring_pass(buf, ss, rs, n):
        ring_copy(buf, ss, rs, n, 0, left, 0, rows, right).wait_recv()
        ring_copy(buf, ss, rs, n, 2, left, 0, half, right).start()
        ring_copy(buf, ss, rs, n, 1, right, 0, rows, left).wait_recv()
        ring_copy(buf, ss, rs, n, 3, right, half, half, left).start()

    def ring_wait(buf, ss, rs, n):
        ring_copy(buf, ss, rs, n, 2, across, 0, half, right).wait_recv()
        ring_copy(buf, ss, rs, n, 3, across, half, half, left).wait_recv()

    def ring_done(buf, ss, rs, n):
        ring_copy(buf, ss, rs, n, 0, x, 0, rows, right).wait_send()
        ring_copy(buf, ss, rs, n, 1, x, 0, rows, left).wait_send()
        ring_copy(buf, ss, rs, n, 2, left, 0, half, right).wait_send()
        ring_copy(buf, ss, rs, n, 3, right, half, half, left).wait_send()

    a_acc[...] = jnp.zeros_like(a_acc)
    u_acc[...] = jnp.zeros_like(u_acc)
    q_acc[...] = jnp.zeros_like(q_acc)

    @pl.loop(0, nc)
    def _(step):
        k = turn(step)
        z_recv(xs, xr, xss, xrs, k)
        share_start(xr, xsl, xa_s, xa_r, k, 0)
        w_copy(0, k).wait()
        w_copy(1, k).wait()

        @pl.loop(0, ff // tile)
        def _(n):
            c = pl.ds(pl.multiple_of(n * tile, tile), tile)
            a_acc[:, c] += nn(xr[k], wg[k, :, c])
            u_acc[:, c] += nn(xr[k], wu[k, :, c])

    a = a_acc[...]
    hh[rows_of(x), :] = (a * jax.nn.sigmoid(a) * u_acc[...]).astype(BF16)
    gather_start(hh, h_s, h_r)

    def pipe_copy(k):
        return mesh_copy(up.at[k], up.at[k], pss.at[k], prs.at[k], p_peer)

    def take_dr(step):
        k = turn(step)
        relayed = is_last & (step >= direct)

        @pl.when(relayed)
        def _():
            hand_up(step - direct).wait_recv()

        @pl.when(jnp.logical_not(relayed))
        def _():
            z_recv(gs, dr, gss, grs, k)

        share_start(dr, dsl, da_s, da_r, k, 1)
        w_copy(2, k).wait()

        @pl.loop(0, ff // tile)
        def _(n):
            c = pl.ds(pl.multiple_of(n * tile, tile), tile)
            q_acc[:, c] += nn(dr[k], wd[k, :, c])

    @pl.loop(0, nc + 1)
    def _(step):
        @pl.when(jnp.logical_not(is_last) & (step < nc))
        def _():
            pipe_copy(turn(step)).wait_recv()
            send_scaled(turn(step))

        @pl.when(step > 0)
        def _():
            take_dr(step - 1)

    a = a_acc[...]
    sg = jax.nn.sigmoid(a)
    q = q_acc[...]
    aa[rows_of(x), :] = (q * u_acc[...] * sg * (1.0 + a * (1.0 - sg))).astype(BF16)
    uu[rows_of(x), :] = (q * (a * sg)).astype(BF16)
    for n in range(pieces):
        ring_start(aa, ag_s, ag_r, n)
    for n in range(pieces):
        ring_start(uu, au_s, au_r, n)


    @pl.loop(0, nc)
    def _(step):
        k = turn(step)
        z_done(xs, xr, xss, xrs, k)
        ga = aa[rows_of(x), :]
        gu = uu[rows_of(x), :]

        @pl.loop(0, cp // tile)
        def _(n):
            c = pl.ds(pl.multiple_of(n * tile, tile), tile)
            xs[k, :, c] = (nt(ga, wg[k, c, :]) + nt(gu, wu[k, c, :])).astype(BF16)

        z_start(xs, ret, dss, drs, k)

    def ig_copy(k):
        return pltpu.make_async_copy(up.at[k], ig_ref.at[:, chunk(k)], igs.at[k])

    def combine():
        @pl.loop(0, nc)
        def _(step):
            k = turn(step)
            z_recv(xs, ret, dss, drs, k)
            up[k] = (up[k].astype(F32) + nn(selt[...], ret[k])).astype(BF16)

            @pl.when(is_last)
            def _():
                pipe_copy(k).start()

            ig_copy(k).start()

    @pl.when(is_last)
    def _():
        combine()

    kh = wg.shape[2] // rows if wg.shape[2] % rows == 0 else 1

    def transposed(src, dst):
        for s in range(NX):
            for h in range(ny):
                dst[s // kh * ny + h, :, (s % kh) * rows : (s % kh + 1) * rows] = (
                    jnp.transpose(src[s, h])
                )

    def columns(n):
        return pl.ds(n * tile, tile)

    def product(lhs, rhs, h, n):
        c = columns(n)
        acc = nn(lhs[h], rhs[0 : kh * rows, c])
        for m in range(1, NX // kh):
            acc += nn(lhs[m * ny + h], rhs[m * kh * rows : (m + 1) * kh * rows, c])
        return acc

    def y_copy(t, n):
        return mesh_copy(
            wd.at[t, :, columns(n)], yrecv.at[t, :, columns(n)],
            ys.at[t, n], yr.at[t, n], y_peer,
        )

    def for_peer(t, lhs, rhs, n):
        wd[t, :, columns(n)] = product(lhs, rhs, lax.rem(yh + 1, ny), n).astype(BF16)
        y_copy(t, n).start()

    def out_copy(t, n):
        out = (od_ref, og_ref, ou_ref)[t]
        return pltpu.make_async_copy(
            wd.at[3 + t, :, columns(n)], out.at[:, columns(n)], gos.at[t, n]
        )

    def for_me(t, lhs, rhs, n):
        mine = product(lhs, rhs, yh, n)
        y_copy(t, n).wait()
        wd[3 + t, :, columns(n)] = (
            mine + yrecv[t, :, columns(n)].astype(F32)
        ).astype(BF16)
        out_copy(t, n).start()

    ring = [(aa, ag_s, ag_r, n) for n in range(pieces)]
    ring += [(uu, au_s, au_r, n) for n in range(pieces)]
    ring_pass(*ring[0])
    share_wait(dr, dsl, da_s, da_r, 1)
    transposed(dsl, wu)
    ring_pass(*ring[1])
    gather_wait(hh, h_s, h_r)
    for n in range(pieces):
        for_peer(0, wu, hh, n)
    ring_pass(*ring[2])
    share_wait(xr, xsl, xa_s, xa_r, 0)
    transposed(xsl, wg)
    for i in range(len(ring)):
        if i + 3 < len(ring):
            ring_pass(*ring[i + 3])
        ring_wait(*ring[i])
        for_peer(1 + i // pieces, wg, ring[i][0], i % pieces)

    @pl.when(jnp.logical_not(is_last))
    def _():
        combine()

    for n in range(pieces):
        for_me(0, wu, hh, n)
    for i in range(len(ring)):
        for_me(1 + i // pieces, wg, ring[i][0], i % pieces)
    for args in ring:
        ring_done(*args)

    @pl.loop(0, nc)
    def _(step):
        k = turn(step)

        @pl.when(jnp.logical_not(is_last) | (step < direct))
        def _():
            z_done(gs, dr, gss, grs, k)

        z_done(xs, ret, dss, drs, k)
        ig_copy(k).wait()

        @pl.when(is_last)
        def _():
            pipe_copy(k).wait_send()

    @pl.when(is_last)
    def _():
        tab_copy.wait_send()

    @pl.when(jnp.logical_not(is_last))
    def _():
        @pl.loop(0, RELAYED)
        def _(m):
            hand_up(m).wait_send()

    for t in range(3):
        for n in range(pieces):
            out_copy(t, n).wait()


def settle(*refs):
    count = (len(refs) - 2) // 3
    ins, outs, held = refs[:count], refs[count : 2 * count], refs[2 * count : 3 * count]
    got, put = refs[-2:]
    loads = [pltpu.make_async_copy(ins[i], held[i], got.at[i]) for i in range(count)]
    stores = [pltpu.make_async_copy(held[i], outs[i], put.at[i]) for i in range(count)]
    for c in loads:
        c.start()
    for load, store in zip(loads, stores):
        load.wait()
        store.start()
    for c in stores:
        c.wait()


def local(
    activations, cotangent, routes, route_weights, placement, gate_weight, up_weight, down_weight
):
    ne = lax.axis_size("expert")
    ny = lax.axis_size("dp") // NX
    _, micro, count, d = activations.shape
    tokens = micro * count
    ff = gate_weight.shape[3]
    rows = ne * micro * CAP
    nc = NX * ny
    cp = d // nc
    vm = functools.partial(pl.BlockSpec, memory_space=pltpu.VMEM)
    hbm = functools.partial(pl.BlockSpec, memory_space=pl.ANY)
    dma = pltpu.SemaphoreType.DMA
    wide = pltpu.VMEM((nc, rows, cp), BF16)
    shares = pltpu.VMEM((NX, ny, rows, cp), BF16)
    tall = pltpu.VMEM((NX * rows, ff), BF16)
    weight = pltpu.VMEM((nc, cp, ff), BF16)
    acc = pltpu.VMEM((rows, ff), F32)
    np_ = ff // 256
    outs = pl.pallas_call(
        functools.partial(mega, micro),
        out_shape=(
            jax.ShapeDtypeStruct((tokens, d), BF16),
            jax.ShapeDtypeStruct((cp, ff), BF16),
            jax.ShapeDtypeStruct((cp, ff), BF16),
            jax.ShapeDtypeStruct((cp, ff), BF16),
        ),
        in_specs=[vm()] * 4 + [pl.BlockSpec(memory_space=pltpu.SMEM)] + [hbm()] * 3,
        out_specs=(hbm(),) * 4,
        scratch_shapes=[
            weight, weight, weight,
            wide, wide, wide, wide, wide,
            pltpu.VMEM((nc, tokens, cp), BF16),
            shares, shares,
            tall, tall, tall,
            pltpu.VMEM((3, cp, ff), BF16),
            pltpu.VMEM((rows, tokens), BF16),
            pltpu.VMEM((tokens, rows), BF16),
            pltpu.VMEM((rows, 128), F32),
            pltpu.VMEM((RELAYED, rows, cp), BF16),
            pltpu.VMEM((tokens, 128), F32),
            pltpu.VMEM((rows, tokens), BF16),
            pltpu.VMEM((rows, 128), F32),
            acc, acc, acc,
            dma((3, nc)),
            dma((nc, ne)), dma((nc, ne)), dma((nc, ne)), dma((nc, ne)),
            dma((nc, ne)), dma((nc, ne)),
            dma((2, ny)),
            dma((nc,)), dma((nc,)),
            dma((nc,)), dma((NX, ny)), dma((nc,)), dma((NX, ny)),
            dma((NX,)), dma((NX,)), dma((np_, 4)), dma((np_, 4)), dma((np_, 4)), dma((np_, 4)),
            dma((3, np_)), dma((3, np_)), dma((nc,)), dma((3, np_)),
            dma((RELAYED, ne)), dma((RELAYED, ne)), dma((RELAYED,)), dma((RELAYED,)),
            dma((1,)), dma((1,)),
        ],
        compiler_params=pltpu.CompilerParams(
            collective_id=0, has_side_effects=True, vmem_limit_bytes=63 * 2**20
        ),
        cost_estimate=pl.CostEstimate(
            flops=20 * 10**9, bytes_accessed=24 * 10**6, transcendentals=10**6
        ),
    )(
        activations.reshape(tokens, d),
        cotangent.reshape(tokens, d),
        routes.reshape(tokens, -1),
        route_weights.reshape(tokens, -1),
        placement,
        gate_weight[0, 0],
        up_weight[0, 0],
        down_weight[0, 0],
    )
    outs = pl.pallas_call(
        settle,
        out_shape=tuple(jax.ShapeDtypeStruct(o.shape, o.dtype) for o in outs),
        in_specs=[hbm()] * 4,
        out_specs=(hbm(),) * 4,
        scratch_shapes=[pltpu.VMEM(o.shape, o.dtype) for o in outs] + [dma((4,)), dma((4,))],
    )(*outs)
    return (
        outs[0].reshape(1, micro, count, d),
        outs[1][None, None],
        outs[2][None, None],
        outs[3][None, None],
    )


def solution(mesh):
    blocks = ("expert", "dp")
    placed = (
        P("pipe", None, blocks, None),
        P(None, blocks, None),
        P("pipe", None, blocks, None),
        P("pipe", None, blocks, None),
        P("pipe", None),
        P("pipe", "expert", None, None),
        P("pipe", "expert", None, None),
        P("pipe", "expert", None, None),
    )
    return jax.shard_map(
        local,
        mesh=mesh,
        in_specs=placed,
        out_specs=(
            P("pipe", None, blocks, None),
            P("pipe", "expert", "dp", None),
            P("pipe", "expert", "dp", None),
            P("pipe", "expert", "dp", None),
        ),
        check_vma=False,
    )
```

```python
import functools

import jax
import jax.numpy as jnp
from jax import lax
from jax.experimental import pallas as pl
from jax.experimental.pallas import tpu as pltpu
from jax.sharding import PartitionSpec as P

CAP = 24
RELAYED = 4
NX = 4
F32 = jnp.float32
BF16 = jnp.bfloat16


def nt(left, right):
    return lax.dot_general(left, right, (((1,), (1,)), ((), ())), preferred_element_type=F32)


def nn(left, right):
    return jnp.dot(left, right, preferred_element_type=F32)


def mega(
    micro, x_ref, cot_ref, routes_ref, rw_ref, place_ref, wg_hbm, wu_hbm, wd_hbm,
    ig_ref, og_ref, ou_ref, od_ref,
    wg, wu, wd, xs, gs, xr, dr, ret, up, xsl, dsl, hh, aa, uu, yrecv,
    sel, selt, scale, rel, tab, sel1, scale1, a_acc, u_acc, q_acc,
    wsem, xss, xrs, gss, grs, dss, drs, lsem, pss, prs,
    xa_s, xa_r, da_s, da_r, h_s, h_r, ag_s, ag_r, au_s, au_r, ys, yr, igs, gos,
    rls, rlr, fws, fwr, tbs, tbr,
):
    p = lax.axis_index("pipe")
    me = lax.axis_index("expert")
    j = lax.axis_index("dp")
    ne = lax.axis_size("expert")
    ndp = lax.axis_size("dp")
    ny = ndp // NX
    x = lax.rem(j, NX)
    yh = j // NX
    last = lax.axis_size("pipe") - 1
    tokens, d = x_ref.shape
    rows = sel.shape[0]
    blk = rows // ne
    ff = wg.shape[2]
    nc = ndp
    cp = d // nc
    is_last = p == last

    def at_z(e):
        return (p, e, j)

    def at_x(k):
        return (p, me, yh * NX + k)

    def mesh_copy(src, dst, s, r, dev):
        return pltpu.make_async_remote_copy(
            src_ref=src, dst_ref=dst, send_sem=s, recv_sem=r,
            device_id=dev, device_id_type=pl.DeviceIdType.MESH,
        )

    def chunk(k):
        return pl.ds(pl.multiple_of(k * cp, cp), cp)

    y_peer = (p, me, lax.rem(yh + 1, ny) * NX + x)
    p_peer = (last - p, me, j)

    def w_copy(t, k):
        src, dst = ((wg_hbm, wg), (wu_hbm, wu), (wd_hbm, wd))[t]
        return pltpu.make_async_copy(src.at[chunk(k)], dst.at[k], wsem.at[t, k])

    for t in range(3):
        for k in range(nc):
            w_copy(t, k).start()

    barrier = pltpu.get_barrier_semaphore()
    peers = [at_z(lax.rem(me + o, ne)) for o in range(1, ne)]
    peers += [at_x(lax.rem(x + o, NX)) for o in range(1, NX)]
    peers += [y_peer, p_peer]
    for dev in peers:
        pl.semaphore_signal(barrier, inc=1, device_id=dev, device_id_type=pl.DeviceIdType.MESH)

    square = (tokens, tokens)
    t_row = lax.broadcasted_iota(jnp.int32, square, 0)
    t_col = lax.broadcasted_iota(jnp.int32, square, 1)
    count = tokens // micro
    before = (t_col < t_row) & (t_col // count == t_row // count)
    micro_of = (lax.broadcasted_iota(jnp.int32, (tokens, 1), 0) // count).astype(F32)

    def as_row(column):
        return jnp.transpose(jnp.broadcast_to(column, square))[0:1, :]

    def tables(slots, weights, sel, scale):
        by_col = [jnp.broadcast_to(slots[k], square) for k in range(2)]
        by_row = [jnp.transpose(v) for v in by_col]
        places = []
        for k in range(2):
            same = jnp.where(by_col[0] == by_row[k], 1.0, 0.0) + jnp.where(
                by_col[1] == by_row[k], 1.0, 0.0
            )
            rank = jnp.sum(jnp.where(before, same, 0.0), axis=1, keepdims=True)
            places.append(by_row[k][:, 0:1] * blk + micro_of * CAP + rank)
        r_iota = lax.broadcasted_iota(jnp.int32, (rows, tokens), 0).astype(F32)
        hits = [r_iota == as_row(v) for v in places]
        sel[...] = jnp.where(hits[0] | hits[1], 1.0, 0.0).astype(BF16)
        weight = sum(jnp.where(hits[k], weights[k], 0.0) for k in range(2))
        scale[...] = jnp.broadcast_to(jnp.sum(weight, axis=1, keepdims=True), scale.shape)
        return places

    def in_row(ref, k):
        return jnp.concatenate([ref[k, m : m + 1, :] for m in range(micro)], axis=1)

    slots, weights = [], []
    for k in range(2):
        ids = in_row(routes_ref, k)
        slot = jnp.zeros(ids.shape, jnp.int32)
        for s in range(ne):
            slot = jnp.where(ids == place_ref[0, s], s, slot)
        slots.append(slot.astype(F32))
        weights.append(in_row(rw_ref, k))

    @pl.when(is_last)
    def _():
        packed = jnp.zeros(tab.shape, F32)
        line = lax.broadcasted_iota(jnp.int32, tab.shape, 0)
        for n, row in enumerate(slots + weights):
            packed = jnp.where(line == n, row, packed)
        tab[...] = packed

    tab_copy = mesh_copy(tab, tab, tbs.at[0], tbr.at[0], p_peer)

    pl.semaphore_wait(barrier, len(peers))

    @pl.when(is_last)
    def _():
        tab_copy.start()

    places = tables(slots, weights, sel, scale)
    c_iota = lax.broadcasted_iota(jnp.int32, (tokens, rows), 1).astype(F32)
    selt[...] = jnp.where((c_iota == places[0]) | (c_iota == places[1]), 1.0, 0.0).astype(BF16)

    def my_rows(e):
        return pl.ds(pl.multiple_of(e * blk, 16), blk)

    def z_sends(stage, land, ss, rs, k):
        out = []
        for o in range(1, ne):
            e = lax.rem(me + o, ne)
            out.append(
                mesh_copy(
                    stage.at[k, my_rows(e)], land.at[k, my_rows(me)],
                    ss.at[k, o], rs.at[k, o], at_z(e),
                )
            )
        return out

    def z_own(stage, land, ss, k):
        return pltpu.make_async_copy(
            stage.at[k, my_rows(me)], land.at[k, my_rows(me)], ss.at[k, 0]
        )

    def z_start(stage, land, ss, rs, k):
        for c in z_sends(stage, land, ss, rs, k):
            c.start()
        z_own(stage, land, ss, k).start()

    def z_recv(stage, land, ss, rs, k):
        for o in range(1, ne):
            e = lax.rem(me + ne - o, ne)
            mesh_copy(
                stage.at[k, my_rows(e)], land.at[k, my_rows(e)],
                ss.at[k, o], rs.at[k, o], at_z(e),
            ).wait_recv()
        z_own(stage, land, ss, k).wait()

    def z_done(stage, land, ss, rs, k):
        for c in z_sends(stage, land, ss, rs, k):
            c.wait_send()

    def send_scaled(k):
        picked = nn(sel[...], up[k])
        gs[k] = (scale[:, 0:1] * picked).astype(BF16)
        z_start(gs, dr, gss, grs, k)

    def turn(step):
        own = step // (2 * NX - 2)
        r = lax.rem(step, 3)
        o = (1 - own) * (1 + 2 * r - 3 * (r // 2))
        h = (1 - own) * (step // 3) + own * (step - (2 * NX - 2))
        return h * NX + lax.rem(x + o, NX)

    direct = nc - RELAYED

    def relay_copy(m, o):
        e = lax.rem(me + o, ne)
        return mesh_copy(
            gs.at[turn(direct + m), my_rows(e)], rel.at[m, my_rows(me)],
            rls.at[m, o], rlr.at[m, o], at_z(e),
        )

    def relay_own(m):
        return pltpu.make_async_copy(
            gs.at[turn(direct + m), my_rows(me)], rel.at[m, my_rows(me)], rls.at[m, 0]
        )

    def hand_up(m):
        return mesh_copy(rel.at[m], dr.at[turn(direct + m)], fws.at[m], fwr.at[m], p_peer)

    def send_inputs(step):
        k = turn(step)
        xs[k] = nn(sel[...], x_ref[:, chunk(k)]).astype(BF16)
        z_start(xs, xr, xss, xrs, k)

        @pl.when(is_last)
        def _():
            up[k] = cot_ref[:, chunk(k)]

        @pl.when(is_last & (step < direct))
        def _():
            send_scaled(k)

    @pl.loop(0, 2)
    def _(step):
        send_inputs(step)

    @pl.when(jnp.logical_not(is_last))
    def _():
        tab_copy.wait_recv()
        held = [tab[n : n + 1, :] for n in range(4)]
        tables(held[0:2], held[2:4], sel1, scale1)

        @pl.loop(0, RELAYED)
        def _(m):
            k = turn(direct + m)
            picked = nn(sel1[...], cot_ref[:, chunk(k)])
            gs[k] = (scale1[:, 0:1] * picked).astype(BF16)
            for o in range(1, ne):
                relay_copy(m, o).start()
            relay_own(m).start()

    @pl.loop(2, nc)
    def _(step):
        send_inputs(step)

    @pl.when(jnp.logical_not(is_last))
    def _():
        @pl.loop(0, RELAYED)
        def _(m):
            for o in range(1, ne):
                e = lax.rem(me + ne - o, ne)
                mesh_copy(
                    gs.at[turn(direct + m), my_rows(e)], rel.at[m, my_rows(e)],
                    rls.at[m, o], rlr.at[m, o], at_z(e),
                ).wait_recv()
            relay_own(m).wait()
            hand_up(m).start()
            for o in range(1, ne):
                relay_copy(m, o).wait_send()

    def share_copy(src, dst, ss, rs, k):
        return mesh_copy(
            src.at[k], dst.at[x, k // NX], ss.at[k], rs.at[x, k // NX], at_x(lax.rem(k, NX))
        )

    def share_local(src, dst, k, n):
        return pltpu.make_async_copy(src.at[k], dst.at[x, k // NX], lsem.at[n, k // NX])

    def share_start(src, dst, ss, rs, k, n):
        @pl.when(lax.rem(k, NX) != x)
        def _():
            share_copy(src, dst, ss, rs, k).start()

        @pl.when(lax.rem(k, NX) == x)
        def _():
            share_local(src, dst, k, n).start()

    def share_wait(src, dst, ss, rs, n):
        for h in range(ny):
            for o in range(1, NX):
                s = lax.rem(x + o, NX)
                k = h * NX + s
                share_copy(src, dst, ss, rs, k).wait_send()
                mesh_copy(src.at[k], dst.at[s, h], ss.at[k], rs.at[s, h], at_x(s)).wait_recv()
            share_local(src, dst, h * NX + x, n).wait()

    def rows_of(s):
        return pl.ds(pl.multiple_of(s * rows, 16), rows)

    def gather(buf, ss, rs):
        return [
            mesh_copy(
                buf.at[rows_of(x)], buf.at[rows_of(x)], ss.at[o], rs.at[o],
                at_x(lax.rem(x + o, NX)),
            )
            for o in range(1, NX)
        ]

    def gather_start(buf, ss, rs):
        for c in gather(buf, ss, rs):
            c.start()

    def gather_wait(buf, ss, rs):
        for o, c in zip(range(1, NX), gather(buf, ss, rs)):
            c.wait_send()
            s = lax.rem(x + NX - o, NX)
            mesh_copy(
                buf.at[rows_of(s)], buf.at[rows_of(s)], ss.at[o], rs.at[o], at_x(s)
            ).wait_recv()

    tile = 256

    pieces = ff // tile
    half = rows // 2
    right, left = lax.rem(x + 1, NX), lax.rem(x + NX - 1, NX)
    across = lax.rem(x + 2, NX)

    def ring_copy(buf, ss, rs, n, way, owner, first, count, to):
        part = buf.at[
            pl.ds(pl.multiple_of(owner * rows + first, 16), count), pl.ds(n * tile, tile)
        ]
        return mesh_copy(part, part, ss.at[n, way], rs.at[n, way], at_x(to))

    def ring_start(buf, ss, rs, n):
        ring_copy(buf, ss, rs, n, 0, x, 0, rows, right).start()
        ring_copy(buf, ss, rs, n, 1, x, 0, rows, left).start()

    def ring_pass(buf, ss, rs, n):
        ring_copy(buf, ss, rs, n, 0, left, 0, rows, right).wait_recv()
        ring_copy(buf, ss, rs, n, 2, left, 0, half, right).start()
        ring_copy(buf, ss, rs, n, 1, right, 0, rows, left).wait_recv()
        ring_copy(buf, ss, rs, n, 3, right, half, half, left).start()

    def ring_wait(buf, ss, rs, n):
        ring_copy(buf, ss, rs, n, 2, across, 0, half, right).wait_recv()
        ring_copy(buf, ss, rs, n, 3, across, half, half, left).wait_recv()

    def ring_done(buf, ss, rs, n):
        ring_copy(buf, ss, rs, n, 0, x, 0, rows, right).wait_send()
        ring_copy(buf, ss, rs, n, 1, x, 0, rows, left).wait_send()
        ring_copy(buf, ss, rs, n, 2, left, 0, half, right).wait_send()
        ring_copy(buf, ss, rs, n, 3, right, half, half, left).wait_send()

    a_acc[...] = jnp.zeros_like(a_acc)
    u_acc[...] = jnp.zeros_like(u_acc)
    q_acc[...] = jnp.zeros_like(q_acc)

    @pl.loop(0, nc)
    def _(step):
        k = turn(step)
        z_recv(xs, xr, xss, xrs, k)
        share_start(xr, xsl, xa_s, xa_r, k, 0)
        w_copy(0, k).wait()
        w_copy(1, k).wait()

        @pl.loop(0, ff // tile)
        def _(n):
            c = pl.ds(pl.multiple_of(n * tile, tile), tile)
            a_acc[:, c] += nn(xr[k], wg[k, :, c])
            u_acc[:, c] += nn(xr[k], wu[k, :, c])

    a = a_acc[...]
    hh[rows_of(x), :] = (a * jax.nn.sigmoid(a) * u_acc[...]).astype(BF16)
    gather_start(hh, h_s, h_r)

    def pipe_copy(k):
        return mesh_copy(up.at[k], up.at[k], pss.at[k], prs.at[k], p_peer)

    def take_dr(step):
        k = turn(step)
        relayed = is_last & (step >= direct)

        @pl.when(relayed)
        def _():
            hand_up(step - direct).wait_recv()

        @pl.when(jnp.logical_not(relayed))
        def _():
            z_recv(gs, dr, gss, grs, k)

        share_start(dr, dsl, da_s, da_r, k, 1)
        w_copy(2, k).wait()

        @pl.loop(0, ff // tile)
        def _(n):
            c = pl.ds(pl.multiple_of(n * tile, tile), tile)
            q_acc[:, c] += nn(dr[k], wd[k, :, c])

    @pl.loop(0, nc + 1)
    def _(step):
        @pl.when(jnp.logical_not(is_last) & (step < nc))
        def _():
            pipe_copy(turn(step)).wait_recv()
            send_scaled(turn(step))

        @pl.when(step > 0)
        def _():
            take_dr(step - 1)

    a = a_acc[...]
    sg = jax.nn.sigmoid(a)
    q = q_acc[...]
    aa[rows_of(x), :] = (q * u_acc[...] * sg * (1.0 + a * (1.0 - sg))).astype(BF16)
    uu[rows_of(x), :] = (q * (a * sg)).astype(BF16)
    for n in range(pieces):
        ring_start(aa, ag_s, ag_r, n)
    for n in range(pieces):
        ring_start(uu, au_s, au_r, n)


    @pl.loop(0, nc)
    def _(step):
        k = turn(step)
        z_done(xs, xr, xss, xrs, k)
        ga = aa[rows_of(x), :]
        gu = uu[rows_of(x), :]

        @pl.loop(0, cp // tile)
        def _(n):
            c = pl.ds(pl.multiple_of(n * tile, tile), tile)
            xs[k, :, c] = (nt(ga, wg[k, c, :]) + nt(gu, wu[k, c, :])).astype(BF16)

        z_start(xs, ret, dss, drs, k)

    def ig_copy(k):
        return pltpu.make_async_copy(up.at[k], ig_ref.at[:, chunk(k)], igs.at[k])

    def combine():
        @pl.loop(0, nc)
        def _(step):
            k = turn(step)
            z_recv(xs, ret, dss, drs, k)
            up[k] = (up[k].astype(F32) + nn(selt[...], ret[k])).astype(BF16)

            @pl.when(is_last)
            def _():
                pipe_copy(k).start()

            ig_copy(k).start()

    @pl.when(is_last)
    def _():
        combine()

    kh = wg.shape[2] // rows if wg.shape[2] % rows == 0 else 1

    def transposed(src, dst):
        for s in range(NX):
            for h in range(ny):
                dst[s // kh * ny + h, :, (s % kh) * rows : (s % kh + 1) * rows] = (
                    jnp.transpose(src[s, h])
                )

    def columns(n):
        return pl.ds(n * tile, tile)

    def part(v):
        return pl.ds(v * (cp // 2), cp // 2)

    def product(lhs, rhs, h, n, v):
        c = columns(n)
        acc = nn(lhs[h, part(v)], rhs[0 : kh * rows, c])
        for m in range(1, NX // kh):
            acc += nn(lhs[m * ny + h, part(v)], rhs[m * kh * rows : (m + 1) * kh * rows, c])
        return acc

    def y_copy(t, n, v):
        return mesh_copy(
            wd.at[t, part(v), columns(n)], yrecv.at[t, part(v), columns(n)],
            ys.at[t, 2 * n + v], yr.at[t, 2 * n + v], y_peer,
        )

    def for_peer(t, lhs, rhs, n):
        for v in range(2):
            wd[t, part(v), columns(n)] = product(lhs, rhs, lax.rem(yh + 1, ny), n, v).astype(BF16)
            y_copy(t, n, v).start()

    def out_copy(t, n):
        out = (od_ref, og_ref, ou_ref)[t]
        return pltpu.make_async_copy(
            wd.at[3 + t, :, columns(n)], out.at[:, columns(n)], gos.at[t, n]
        )

    def for_me(t, lhs, rhs, n):
        for v in range(2):
            mine = product(lhs, rhs, yh, n, v)
            y_copy(t, n, v).wait()
            wd[3 + t, part(v), columns(n)] = (
                mine + yrecv[t, part(v), columns(n)].astype(F32)
            ).astype(BF16)
        out_copy(t, n).start()

    ring = [(aa, ag_s, ag_r, n) for n in range(pieces)]
    ring += [(uu, au_s, au_r, n) for n in range(pieces)]
    ring_pass(*ring[0])
    share_wait(dr, dsl, da_s, da_r, 1)
    transposed(dsl, wu)
    ring_pass(*ring[1])
    gather_wait(hh, h_s, h_r)
    for n in range(pieces):
        for_peer(0, wu, hh, n)
    ring_pass(*ring[2])
    share_wait(xr, xsl, xa_s, xa_r, 0)
    transposed(xsl, wg)
    for i in range(len(ring)):
        if i + 3 < len(ring):
            ring_pass(*ring[i + 3])
        ring_wait(*ring[i])
        for_peer(1 + i // pieces, wg, ring[i][0], i % pieces)

    @pl.when(jnp.logical_not(is_last))
    def _():
        combine()

    for n in range(pieces):
        for_me(0, wu, hh, n)
    for i in range(len(ring)):
        for_me(1 + i // pieces, wg, ring[i][0], i % pieces)
    for args in ring:
        ring_done(*args)

    @pl.loop(0, nc)
    def _(step):
        k = turn(step)

        @pl.when(jnp.logical_not(is_last) | (step < direct))
        def _():
            z_done(gs, dr, gss, grs, k)

        z_done(xs, ret, dss, drs, k)
        ig_copy(k).wait()

        @pl.when(is_last)
        def _():
            pipe_copy(k).wait_send()

    @pl.when(is_last)
    def _():
        tab_copy.wait_send()

    @pl.when(jnp.logical_not(is_last))
    def _():
        @pl.loop(0, RELAYED)
        def _(m):
            hand_up(m).wait_send()

    for t in range(3):
        for n in range(pieces):
            out_copy(t, n).wait()


def settle(*refs):
    count = (len(refs) - 2) // 3
    ins, outs, held = refs[:count], refs[count : 2 * count], refs[2 * count : 3 * count]
    got, put = refs[-2:]
    loads = [pltpu.make_async_copy(ins[i], held[i], got.at[i]) for i in range(count)]
    stores = [pltpu.make_async_copy(held[i], outs[i], put.at[i]) for i in range(count)]
    for c in loads:
        c.start()
    for load, store in zip(loads, stores):
        load.wait()
        store.start()
    for c in stores:
        c.wait()


def local(
    activations, cotangent, routes, route_weights, placement, gate_weight, up_weight, down_weight
):
    ne = lax.axis_size("expert")
    ny = lax.axis_size("dp") // NX
    _, micro, count, d = activations.shape
    tokens = micro * count
    ff = gate_weight.shape[3]
    rows = ne * micro * CAP
    nc = NX * ny
    cp = d // nc
    vm = functools.partial(pl.BlockSpec, memory_space=pltpu.VMEM)
    hbm = functools.partial(pl.BlockSpec, memory_space=pl.ANY)
    dma = pltpu.SemaphoreType.DMA
    wide = pltpu.VMEM((nc, rows, cp), BF16)
    shares = pltpu.VMEM((NX, ny, rows, cp), BF16)
    tall = pltpu.VMEM((NX * rows, ff), BF16)
    weight = pltpu.VMEM((nc, cp, ff), BF16)
    acc = pltpu.VMEM((rows, ff), F32)
    np_ = ff // 256
    outs = pl.pallas_call(
        functools.partial(mega, micro),
        out_shape=(
            jax.ShapeDtypeStruct((tokens, d), BF16),
            jax.ShapeDtypeStruct((cp, ff), BF16),
            jax.ShapeDtypeStruct((cp, ff), BF16),
            jax.ShapeDtypeStruct((cp, ff), BF16),
        ),
        in_specs=[vm()] * 4 + [pl.BlockSpec(memory_space=pltpu.SMEM)] + [hbm()] * 3,
        out_specs=(hbm(),) * 4,
        scratch_shapes=[
            weight, weight, weight,
            wide, wide, wide, wide, wide,
            pltpu.VMEM((nc, tokens, cp), BF16),
            shares, shares,
            tall, tall, tall,
            pltpu.VMEM((3, cp, ff), BF16),
            pltpu.VMEM((rows, tokens), BF16),
            pltpu.VMEM((tokens, rows), BF16),
            pltpu.VMEM((rows, 128), F32),
            pltpu.VMEM((RELAYED, rows, cp), BF16),
            pltpu.VMEM((8, tokens), F32),
            pltpu.VMEM((rows, tokens), BF16),
            pltpu.VMEM((rows, 128), F32),
            acc, acc, acc,
            dma((3, nc)),
            dma((nc, ne)), dma((nc, ne)), dma((nc, ne)), dma((nc, ne)),
            dma((nc, ne)), dma((nc, ne)),
            dma((2, ny)),
            dma((nc,)), dma((nc,)),
            dma((nc,)), dma((NX, ny)), dma((nc,)), dma((NX, ny)),
            dma((NX,)), dma((NX,)), dma((np_, 4)), dma((np_, 4)), dma((np_, 4)), dma((np_, 4)),
            dma((3, 2 * np_)), dma((3, 2 * np_)), dma((nc,)), dma((3, np_)),
            dma((RELAYED, ne)), dma((RELAYED, ne)), dma((RELAYED,)), dma((RELAYED,)),
            dma((1,)), dma((1,)),
        ],
        compiler_params=pltpu.CompilerParams(
            collective_id=0, has_side_effects=True, vmem_limit_bytes=63 * 2**20
        ),
        cost_estimate=pl.CostEstimate(
            flops=20 * 10**9, bytes_accessed=24 * 10**6, transcendentals=10**6
        ),
    )(
        activations.reshape(tokens, d),
        cotangent.reshape(tokens, d),
        jnp.transpose(routes[0], (2, 0, 1)),
        jnp.transpose(route_weights[0], (2, 0, 1)),
        placement,
        gate_weight[0, 0],
        up_weight[0, 0],
        down_weight[0, 0],
    )
    outs = pl.pallas_call(
        settle,
        out_shape=tuple(jax.ShapeDtypeStruct(o.shape, o.dtype) for o in outs),
        in_specs=[hbm()] * 4,
        out_specs=(hbm(),) * 4,
        scratch_shapes=[pltpu.VMEM(o.shape, o.dtype) for o in outs] + [dma((4,)), dma((4,))],
    )(*outs)
    return (
        outs[0].reshape(1, micro, count, d),
        outs[1][None, None],
        outs[2][None, None],
        outs[3][None, None],
    )


def solution(mesh):
    blocks = ("expert", "dp")
    placed = (
        P("pipe", None, blocks, None),
        P(None, blocks, None),
        P("pipe", None, blocks, None),
        P("pipe", None, blocks, None),
        P("pipe", None),
        P("pipe", "expert", None, None),
        P("pipe", "expert", None, None),
        P("pipe", "expert", None, None),
    )
    return jax.shard_map(
        local,
        mesh=mesh,
        in_specs=placed,
        out_specs=(
            P("pipe", None, blocks, None),
            P("pipe", "expert", "dp", None),
            P("pipe", "expert", "dp", None),
            P("pipe", "expert", "dp", None),
        ),
        check_vma=False,
    )
```
